32 devices in a mesh: ctx: 8 (over z, x), head: 4 (over y, core).
Axes of the slice: x: 2, y: 2, z: 4, core: 2. Of those that a mesh axis runs over, the one named last changes fastest.
Arguments:
- queries: bfloat16 [512, 16, 128], P('ctx', 'head'), may hold values from -9 to 9
- cache_keys: bfloat16 [16384, 128], P('ctx'), may hold values from -15 to 15
- cache_values: bfloat16 [16384, 128], P('ctx'), may hold values from -6 to 6
- page_table: int32 [8, 4], P('ctx'), may hold values from 0 to 3, each once within a row
- page_count: int32 [8], P('ctx'), may hold values from 1 to 4, as said below
- new_kv: bfloat16 [512, 2, 128], P(('ctx', 'head')), may hold values from -15 to 15
- new_owner: int32 [512], replicated, may hold values from 0 to 7, as said below
- new_offset: int32 [512], replicated, may hold values from 0 to 127
Outputs:
- attended: bfloat16 [512, 16, 128], P('ctx', 'head')
- appended: bfloat16 [1024, 2, 128], P('ctx')
The draws below stay inside these ranges and needn't reach their ends.
Inputs may be any that keep to these rules, and one draw needn't show every extreme that they name: `page_count`: some store has all 4 pages live. `page_table`: each row names every page once. `new_owner`: no two new tokens share a pair of owner and offset; some store's 128 rows are all taken.
All inputs are finite; a program needn't handle non-finite values.
Results may differ from the reference program's by a relative error of at most 0.0028.
Values may be sent and summed in bfloat16 or wider, within the bound.
A program may use at most 64 MiB of HBM per device.

```python
import math
import jax
import jax.numpy as jnp
from jax import lax

HEADS = 16
HD = 128
PAGE = 512
SLOTS = 4
NEW = 512
APPEND = 128
CACHE_ROWS = 16384
N_CTX = 8


def owner_slots(key):
    total = N_CTX * APPEND
    first, second, third = jax.random.split(jax.random.fold_in(key, 104), 3)
    fullest = jax.random.randint(first, (), 0, N_CTX)
    ranks = jax.random.permutation(second, total)
    owners = jnp.arange(total) // APPEND
    ranks = jnp.where(owners == fullest, ranks - total, ranks)
    order = jnp.argsort(ranks, stable=True)
    chosen = jax.random.permutation(third, order[:NEW])
    return chosen.astype(jnp.int32)


def draw_queries(key, part):
    key = jax.random.fold_in(key, 1)
    result = 1.5 * jax.random.truncated_normal(key, -6.0, 6.0, (NEW, HEADS, HD))
    return result.astype(jnp.bfloat16)


def draw_new_kv(key, part):
    key = jax.random.fold_in(key, 2)
    first, second = jax.random.split(key)
    key_rows = 2.5 * jax.random.truncated_normal(first, -6.0, 6.0, (NEW, HD))
    value_rows = jax.random.truncated_normal(second, -6.0, 6.0, (NEW, HD))
    return jnp.stack([key_rows, value_rows], axis=1).astype(jnp.bfloat16)


def draw_page_count(key, part):
    key = jax.random.fold_in(key, 3)
    first, second = jax.random.split(key)
    counts = jax.random.randint(first, (N_CTX,), 1, SLOTS // 2 + 1)
    fullest = jax.random.randint(second, (), 0, N_CTX)
    return counts.at[fullest].set(SLOTS).astype(jnp.int32)


def draw_new_owner(key, part):
    chosen = owner_slots(key)
    return (chosen // APPEND).astype(jnp.int32)


def draw_new_offset(key, part):
    chosen = owner_slots(key)
    return (chosen % APPEND).astype(jnp.int32)


def block_levels(stream_key, shape, cuts, smallest, high):
    level, own = 1.0, jax.random.fold_in(stream_key, 6)
    for axis_at, shards_of in cuts:
        steps = jnp.exp(jax.random.uniform(jax.random.fold_in(own, axis_at), (shards_of,), jnp.float32, smallest / len(cuts), high / len(cuts)))
        level = level * jnp.repeat(steps, shape[axis_at] // shards_of).reshape([-1 if axis == axis_at else 1 for axis in range(len(shape))])
    return level


def normal_values(rng, extent, scale, limit, cuts=(), held_as=jnp.bfloat16):
    values = scale * jax.random.normal(rng, extent, jnp.float32)
    if cuts:
        values = values * block_levels(rng, extent, cuts, -0.22, 0.18)
    return jnp.clip(values, -limit, limit).astype(held_as)


def setup_inputs(seed: int = 0) -> dict:
    splits = jax.random.split(jax.random.key(seed), 9)
    queries = draw_queries(jax.random.fold_in(splits[8], 71), 0)
    cache_keys = normal_values(splits[1], (CACHE_ROWS, HD), 2.5, 15.0, ((0, 8),))
    cache_values = normal_values(splits[2], (CACHE_ROWS, HD), 1.0, 6.0, ((0, 8),))
    page_table = jax.vmap(lambda own: jax.random.permutation(own, SLOTS))(jax.random.split(splits[3], N_CTX)).reshape((N_CTX, SLOTS)).astype(jnp.int32)
    page_count = draw_page_count(jax.random.fold_in(splits[8], 71), 0)
    new_kv = draw_new_kv(jax.random.fold_in(splits[8], 71), 0)
    new_owner = draw_new_owner(jax.random.fold_in(splits[8], 71), 0)
    new_offset = draw_new_offset(jax.random.fold_in(splits[8], 71), 0)
    return dict(queries=queries, cache_keys=cache_keys, cache_values=cache_values, page_table=page_table, page_count=page_count, new_kv=new_kv, new_owner=new_owner, new_offset=new_offset)


def block_partial(scores, values):
    maxima = lax.optimization_barrier(jnp.max(scores, axis=1))
    weights = jnp.exp(scores - maxima[:, None])
    totals = lax.optimization_barrier(jnp.sum(weights, axis=1))
    summed = jnp.dot(weights.astype(jnp.bfloat16), values, preferred_element_type=jnp.float32)
    return (maxima, totals, summed)

def join_partials(first, second):
    combined = jnp.maximum(first[0], second[0])
    factor_one = jnp.exp(first[0] - combined)
    factor_two = jnp.exp(second[0] - combined)
    totals = first[1] * factor_one + second[1] * factor_two
    summed = first[2] * factor_one[:, None] + second[2] * factor_two[:, None]
    return (combined, totals, summed)

def reference(queries, cache_keys, cache_values, page_table, page_count, new_kv, new_owner, new_offset):
    scaling = 1.0 / math.sqrt(HD)
    query_rows = queries.reshape(NEW * HEADS, HD)
    count_rows = NEW * HEADS
    page_slots = jnp.arange(SLOTS, dtype=jnp.int32)

    def one_store(carry, item):
        store_keys, store_values, table_row, live_count = item
        taken = page_slots < live_count
        page_live = jnp.any((table_row[:, None] == page_slots[None, :]) & taken[:, None], axis=0)
        row_live = jnp.repeat(page_live, PAGE)
        scores = lax.dot_general(query_rows, store_keys, (((1,), (1,)), ((), ())), preferred_element_type=jnp.float32) * scaling
        scores = jnp.where(row_live[None, :], scores, jnp.float32(-1e+30))
        found = block_partial(scores, store_values)
        return (join_partials(carry, found), None)
    initial = (jnp.full((count_rows,), -1e+30, jnp.float32), jnp.zeros((count_rows,), jnp.float32), jnp.zeros((count_rows, HD), jnp.float32))
    stacked = (cache_keys.reshape(N_CTX, SLOTS * PAGE, HD), cache_values.reshape(N_CTX, SLOTS * PAGE, HD), page_table, page_count)
    cache_part, unused = lax.scan(one_store, initial, stacked)
    scores = lax.dot_general(query_rows, new_kv[:, 0], (((1,), (1,)), ((), ())), preferred_element_type=jnp.float32) * scaling
    positions = jnp.arange(count_rows, dtype=jnp.int32) // HEADS
    visible = jnp.arange(NEW, dtype=jnp.int32)[None, :] <= positions[:, None]
    scores = jnp.where(visible, scores, jnp.float32(-1e+30))
    self_part = block_partial(scores, new_kv[:, 1])
    maxima, totals, summed = join_partials(cache_part, self_part)
    attended = (summed / totals[:, None]).reshape(NEW, HEADS, HD).astype(jnp.bfloat16)
    target = (new_owner * APPEND + new_offset).astype(jnp.int32)
    appended = jnp.zeros((N_CTX * APPEND, 2, HD), jnp.bfloat16).at[target].set(new_kv)
    return (attended, appended)
```

```python
import functools
import math

import jax
import jax.numpy as jnp
from jax import lax
from jax.experimental import pallas as pl
from jax.experimental.pallas import tpu as pltpu
from jax.sharding import PartitionSpec as P

MESH = pl.DeviceIdType.MESH
FAR = 1e30
STEPS = 32767.0
TINY = 1e-30
NT = (((1,), (1,)), ((), ()))


def attention_kernel(
    layers,
    heads_axis,
    head_dev,
    slots,
    table_ref,
    count_ref,
    queries_ref,
    keys_ref,
    values_ref,
    new_ref,
    owner_ref,
    offset_ref,
    attended_ref,
    appended_ref,
    k_ref,
    v_ref,
    qz_ref,
    qx_ref,
    own_o,
    own_l,
    sx_o,
    sx_l,
    rx_o,
    rx_l,
    sz_o,
    sz_l,
    rz_o,
    rz_l,
    all_new,
    local_sem,
    qz_send,
    qz_recv,
    qx_send,
    qx_recv,
    xo_send,
    xo_recv,
    xl_send,
    xl_recv,
    zo_send,
    zo_recv,
    zl_send,
    zl_recv,
    nz_send,
    nz_recv,
    nx_send,
    nx_recv,
    nh_send,
    nh_recv,
):
    rows, size = queries_ref.shape
    store_rows = keys_ref.shape[0]
    page = store_rows // slots
    new_tok = new_ref.shape[0] // 2
    scale = math.log2(math.e) / math.sqrt(size)
    store = lax.axis_index("ctx")
    head = lax.axis_index("head")
    z = lax.div(store, 2)
    x = lax.rem(store, 2)
    pair = store + 1 - 2 * x

    def along_z(steps):
        return 2 * lax.rem(z + steps, layers) + x

    def along_head(steps):
        return lax.rem(head + steps, heads_axis)

    load_q = pltpu.make_async_copy(queries_ref, qz_ref.at[0], local_sem.at[0])
    load_k = pltpu.make_async_copy(keys_ref, k_ref, local_sem.at[1])
    load_v = pltpu.make_async_copy(values_ref, v_ref.at[:, pl.ds(0, size)], local_sem.at[2])
    load_q.start()
    load_k.start()
    load_v.start()

    barrier = pltpu.get_barrier_semaphore()
    for steps in range(1, layers):
        pl.semaphore_signal(barrier, inc=1, device_id={"ctx": along_z(steps)}, device_id_type=MESH)
    pl.semaphore_signal(barrier, inc=1, device_id={"ctx": pair}, device_id_type=MESH)
    for steps in range(1, heads_axis):
        pl.semaphore_signal(
            barrier, inc=1, device_id={"head": along_head(steps)}, device_id_type=MESH
        )

    out_row = lax.broadcasted_iota(jnp.int32, (2 * new_tok, 2 * new_tok), 0)
    in_row = lax.broadcasted_iota(jnp.int32, (2 * new_tok, 2 * new_tok), 1)
    wanted = jnp.where(out_row < new_tok, 2 * out_row, 2 * (out_row - new_tok) + 1)
    order = jnp.where(in_row == wanted, 1.0, 0.0).astype(jnp.bfloat16)
    all_new[z, x, head] = jnp.dot(
        order, new_ref[...], preferred_element_type=jnp.float32
    ).astype(jnp.bfloat16)
    v_ref[:, pl.ds(size, size)] = jnp.ones((store_rows, size), jnp.bfloat16)

    pl.semaphore_wait(barrier, layers + heads_axis - 1)

    def remote(src, dst, send_sem, recv_sem, device):
        return pltpu.make_async_remote_copy(
            src_ref=src,
            dst_ref=dst,
            send_sem=send_sem,
            recv_sem=recv_sem,
            device_id=device,
            device_id_type=MESH,
        )

    def send_q(steps):
        slot = layers - steps
        return remote(
            queries_ref,
            qz_ref.at[slot],
            qz_send.at[steps],
            qz_recv.at[slot],
            {"ctx": along_z(steps)},
        )

    def take_q(slot):
        return remote(
            queries_ref, qz_ref.at[slot], qz_send.at[slot], qz_recv.at[slot], {"ctx": along_z(slot)}
        )

    def pass_q(slot):
        return remote(
            qz_ref.at[slot], qx_ref.at[slot], qx_send.at[slot], qx_recv.at[slot], {"ctx": pair}
        )

    first_pass = remote(
        queries_ref, qx_ref.at[0], qx_send.at[0], qx_recv.at[0], {"ctx": pair}
    )

    def cross(slot):
        return (
            remote(sx_o.at[slot], rx_o.at[slot], xo_send.at[slot], xo_recv.at[slot], {"ctx": pair}),
            remote(sx_l.at[slot], rx_l.at[slot], xl_send.at[slot], xl_recv.at[slot], {"ctx": pair}),
        )

    def give_back(steps):
        slot = layers - steps
        device = {"ctx": along_z(steps)}
        return (
            remote(sz_o.at[steps], rz_o.at[slot], zo_send.at[steps], zo_recv.at[slot], device),
            remote(sz_l.at[steps], rz_l.at[slot], zl_send.at[steps], zl_recv.at[slot], device),
        )

    def get_back(slot):
        device = {"ctx": along_z(slot)}
        return (
            remote(sz_o.at[slot], rz_o.at[slot], zo_send.at[slot], zo_recv.at[slot], device),
            remote(sz_l.at[slot], rz_l.at[slot], zl_send.at[slot], zl_recv.at[slot], device),
        )

    def new_z(steps):
        mine = all_new.at[z, x, head]
        return remote(
            mine, mine, nz_send.at[steps], nz_recv.at[layers - steps], {"ctx": along_z(steps)}
        )

    def new_z_taken(slot):
        theirs = all_new.at[lax.rem(z + slot, layers), x, head]
        return remote(theirs, theirs, nz_send.at[slot], nz_recv.at[slot], {"ctx": along_z(slot)})

    def new_x(parity):
        block = all_new.at[:, parity, head]
        return remote(block, block, nx_send, nx_recv, {"ctx": pair})

    def new_h(steps):
        mine = all_new.at[:, :, head]
        return remote(
            mine,
            mine,
            nh_send.at[steps],
            nh_recv.at[heads_axis - steps],
            {"head": along_head(steps)},
        )

    def new_h_taken(slot):
        theirs = all_new.at[:, :, along_head(slot)]
        return remote(
            theirs, theirs, nh_send.at[slot], nh_recv.at[slot], {"head": along_head(slot)}
        )

    first_pass.start()
    for steps in range(1, layers):
        send_q(steps).start()
    for steps in range(1, layers):
        new_z(steps).start()

    dead = []
    for number in range(slots):
        live = jnp.int32(0)
        for place in range(slots):
            hit = (table_ref[0, place] == number) & (place < count_ref[0])
            live = jnp.where(hit, jnp.int32(1), live)
        dead.append(jnp.where(live == 1, jnp.float32(0.0), jnp.float32(FAR)))

    def partial(query_rows):
        scores, top = [], None
        for number in range(slots):
            found = lax.dot_general(
                query_rows,
                k_ref[pl.ds(number * page, page), :],
                NT,
                preferred_element_type=jnp.float32,
            )
            scores.append(found)
            page_top = jnp.max(found, axis=1, keepdims=True) - dead[number]
            top = page_top if top is None else jnp.maximum(top, page_top)
        summed = None
        for number in range(slots):
            weights = jnp.exp2((scores[number] - (top + dead[number])) * scale)
            product = jnp.dot(
                weights.astype(jnp.bfloat16),
                v_ref[pl.ds(number * page, page), :],
                preferred_element_type=jnp.float32,
            )
            summed = product if summed is None else summed + product
        totals = summed[:, size:]
        level = top * scale + jnp.log2(totals)
        return summed[:, :size] / totals, level

    def write(mean, level, mean_ref, level_ref):
        largest = jnp.max(jnp.abs(mean), axis=1, keepdims=True)
        steps = jnp.round(mean * (STEPS / jnp.maximum(largest, TINY)))
        mean_ref[...] = steps.astype(jnp.int32).astype(jnp.int16)
        lane = lax.broadcasted_iota(jnp.int32, (rows, size), 1)
        level_ref[...] = jnp.where(lane == 0, level, largest * (1.0 / STEPS)).T[:8, :]

    def read(mean_ref, level_ref):
        level = jnp.broadcast_to(level_ref[0:1, :], (size, rows)).T
        step = jnp.broadcast_to(level_ref[1:2, :], (size, rows)).T
        return mean_ref[...].astype(jnp.int32).astype(jnp.float32) * step, level

    def merged(parts):
        top = functools.reduce(jnp.maximum, [level for _, level in parts])
        share = [jnp.exp2(level - top) for _, level in parts]
        whole = functools.reduce(jnp.add, share)
        summed = functools.reduce(jnp.add, [one * mean for one, (mean, _) in zip(share, parts)])
        return summed / whole, top + jnp.log2(whole)

    def join_pair(slot):
        for copy in cross(slot):
            copy.wait_recv()
        return merged(
            [
                (own_o[slot], own_l[slot]),
                read(rx_o.at[slot], rx_l.at[slot]),
            ]
        )

    def send_joined(slot):
        mean, level = join_pair(slot)
        write(mean, level, sz_o.at[slot], sz_l.at[slot])
        for copy in give_back(slot):
            copy.start()

    def serve_pair(slot):
        mean, level = partial(qx_ref[slot])
        write(mean, level, sx_o.at[slot], sx_l.at[slot])
        for copy in cross(slot):
            copy.start()

    load_q.wait()
    load_k.wait()
    load_v.wait()
    mean, level = partial(qz_ref[0])
    own_o[0] = mean
    own_l[0] = level

    def layer_step(slot, carry):
        take_q(slot).wait_recv()
        pass_q(slot).start()
        mean, level = partial(qz_ref[slot])
        own_o[slot] = mean
        own_l[slot] = level
        pass_q(slot).wait_recv()
        serve_pair(slot)

        @pl.when(slot == 1)
        def _():
            for other in range(1, layers):
                new_z_taken(other).wait_recv()
            new_x(x).start()

        @pl.when(slot >= 2)
        def _():
            send_joined(slot - 1)

        @pl.when(slot == 2)
        def _():
            new_x(1 - x).wait_recv()
            for steps in range(1, heads_axis):
                new_h(steps).start()

        return carry

    lax.fori_loop(1, layers, layer_step, 0)
    first_pass.wait_recv()
    serve_pair(0)
    send_joined(layers - 1)

    for slot in range(1, heads_axis):
        new_h_taken(slot).wait_recv()
    tokens = layers * 2 * heads_axis * new_tok
    gathered = all_new[...].astype(jnp.float32).reshape(tokens // new_tok, 2, new_tok, size)
    new_keys = gathered[:, 0].reshape(tokens, size).astype(jnp.bfloat16)
    new_values = gathered[:, 1].reshape(tokens, size).astype(jnp.bfloat16)

    mine = owner_ref[...] == store
    target = jnp.where(mine, 2 * offset_ref[...], -2)
    place = lax.broadcasted_iota(jnp.int32, (appended_ref.shape[0], tokens), 0)
    key_rows = jnp.where(place == target, 1.0, 0.0).astype(jnp.bfloat16)
    value_rows = jnp.where(place == target + 1, 1.0, 0.0).astype(jnp.bfloat16)
    appended_ref[...] = (
        jnp.dot(key_rows, new_keys, preferred_element_type=jnp.float32)
        + jnp.dot(value_rows, new_values, preferred_element_type=jnp.float32)
    ).astype(jnp.bfloat16)

    scores = lax.dot_general(qz_ref[0], new_keys, NT, preferred_element_type=jnp.float32)
    column = lax.broadcasted_iota(jnp.int32, (1, tokens), 1) * head_dev - store * rows
    row = lax.broadcasted_iota(jnp.int32, (rows, tokens), 0)
    scores = jnp.where(column <= row, scores, -FAR)
    top = jnp.max(scores, axis=1, keepdims=True)
    weights = jnp.exp2((scores - top) * scale)
    totals = jnp.sum(weights, axis=1, keepdims=True)
    summed = jnp.dot(weights.astype(jnp.bfloat16), new_values, preferred_element_type=jnp.float32)
    self_level = jnp.broadcast_to(top * scale + jnp.log2(totals), (rows, size))
    parts = [(summed / totals, self_level), join_pair(0)]
    for slot in range(1, layers):
        for copy in get_back(slot):
            copy.wait_recv()
        parts.append(read(rz_o.at[slot], rz_l.at[slot]))
    attended_ref[...] = merged(parts)[0].astype(jnp.bfloat16)

    first_pass.wait_send()
    for slot in range(layers):
        for copy in cross(slot):
            copy.wait_send()
        if slot:
            send_q(slot).wait_send()
            pass_q(slot).wait_send()
            new_z(slot).wait_send()
            for copy in give_back(slot):
                copy.wait_send()
    new_x(x).wait_send()
    for steps in range(1, heads_axis):
        new_h(steps).wait_send()


def shards(
    queries, cache_keys, cache_values, page_table, page_count, new_kv, new_owner, new_offset
):
    tok_dev, head_dev, size = queries.shape
    new_tok = new_kv.shape[0]
    slots = page_table.shape[1]
    store_rows = cache_keys.shape[0]
    stores = lax.axis_size("ctx")
    heads_axis = lax.axis_size("head")
    layers = stores // 2
    rows = tok_dev * head_dev
    append_rows = 2 * tok_dev
    tokens = new_owner.shape[0]
    bf16, f32 = jnp.bfloat16, jnp.float32
    vmem = pl.BlockSpec(memory_space=pltpu.VMEM)
    smem = pl.BlockSpec(memory_space=pltpu.SMEM)
    anywhere = pl.BlockSpec(memory_space=pl.ANY)
    mean_block = pltpu.VMEM((layers, rows, size), bf16)
    part_block = pltpu.VMEM((layers, rows, size), jnp.int16)
    level_block = pltpu.VMEM((layers, 8, rows), f32)
    dma = pltpu.SemaphoreType.DMA((layers,))
    attended, appended = pl.pallas_call(
        functools.partial(attention_kernel, layers, heads_axis, head_dev, slots),
        out_shape=(
            jax.ShapeDtypeStruct((rows, size), bf16),
            jax.ShapeDtypeStruct((2 * append_rows, size), bf16),
        ),
        in_specs=[smem, smem, anywhere, anywhere, anywhere, vmem, vmem, vmem],
        out_specs=(vmem, vmem),
        scratch_shapes=[
            pltpu.VMEM((store_rows, size), bf16),
            pltpu.VMEM((store_rows, 2 * size), bf16),
            mean_block,
            mean_block,
            pltpu.VMEM((layers, rows, size), f32),
            pltpu.VMEM((layers, rows, size), f32),
            part_block,
            level_block,
            part_block,
            level_block,
            part_block,
            level_block,
            part_block,
            level_block,
            pltpu.VMEM((layers, 2, heads_axis, 2 * new_tok, size), bf16),
            pltpu.SemaphoreType.DMA((3,)),
        ]
        + [dma] * 14
        + [
            pltpu.SemaphoreType.DMA,
            pltpu.SemaphoreType.DMA,
            pltpu.SemaphoreType.DMA((heads_axis,)),
            pltpu.SemaphoreType.DMA((heads_axis,)),
        ],
        compiler_params=pltpu.CompilerParams(
            collective_id=0, has_side_effects=True, vmem_limit_bytes=40 * 1024 * 1024
        ),
    )(
        page_table,
        page_count,
        queries.reshape(rows, size),
        cache_keys,
        cache_values,
        new_kv.reshape(2 * new_tok, size),
        new_owner.reshape(1, tokens),
        new_offset.reshape(1, tokens),
    )
    return (
        attended.reshape(tok_dev, head_dev, size),
        appended.reshape(append_rows, 2, size),
    )


def solution(mesh):
    in_specs = (
        P("ctx", "head", None),
        P("ctx", None),
        P("ctx", None),
        P("ctx", None),
        P("ctx"),
        P(("ctx", "head"), None, None),
        P(),
        P(),
    )
    out_specs = (P("ctx", "head", None), P("ctx", None, None))
    return jax.shard_map(shards, mesh=mesh, in_specs=in_specs, out_specs=out_specs, check_vma=False)
```

```python
import functools
import math

import jax
import jax.numpy as jnp
from jax import lax
from jax.experimental import pallas as pl
from jax.experimental.pallas import tpu as pltpu
from jax.sharding import PartitionSpec as P

MESH = pl.DeviceIdType.MESH
FAR = 1e30
STEPS = 32767.0
TINY = 1e-30
NT = (((1,), (1,)), ((), ()))


def attention_kernel(
    layers,
    heads_axis,
    head_dev,
    slots,
    table_hbm,
    count_ref,
    queries_ref,
    keys_ref,
    values_ref,
    new_hbm,
    owner_hbm,
    offset_hbm,
    attended_ref,
    appended_ref,
    table_ref,
    new_ref,
    owner_ref,
    offset_ref,
    k_ref,
    kt_ref,
    v_ref,
    qz_ref,
    qx_ref,
    own_o,
    own_l,
    sx_o,
    sx_l,
    rx_o,
    rx_l,
    sz_o,
    sz_l,
    rz_o,
    rz_l,
    all_new,
    local_sem,
    qz_send,
    qz_recv,
    qx_send,
    qx_recv,
    xo_send,
    xo_recv,
    xl_send,
    xl_recv,
    zo_send,
    zo_recv,
    zl_send,
    zl_recv,
    nz_send,
    nz_recv,
    nx_send,
    nx_recv,
    nh_send,
    nh_recv,
):
    rows, size = queries_ref.shape
    store_rows = keys_ref.shape[0]
    page = store_rows // slots
    new_tok = new_hbm.shape[0] // 2
    scale = math.log2(math.e) / math.sqrt(size)
    store = lax.axis_index("ctx")
    head = lax.axis_index("head")
    z = lax.div(store, 2)
    x = lax.rem(store, 2)
    pair = store + 1 - 2 * x

    def along_z(steps):
        return 2 * lax.rem(z + steps, layers) + x

    def along_head(steps):
        return lax.rem(head + steps, heads_axis)

    load_new = pltpu.make_async_copy(new_hbm, new_ref, local_sem.at[3])
    small = [
        pltpu.make_async_copy(table_hbm, table_ref, local_sem.at[4]),
        pltpu.make_async_copy(owner_hbm, owner_ref, local_sem.at[5]),
        pltpu.make_async_copy(offset_hbm, offset_ref, local_sem.at[6]),
    ]
    load_q = pltpu.make_async_copy(queries_ref, qz_ref.at[0], local_sem.at[0])
    load_k = pltpu.make_async_copy(keys_ref, k_ref, local_sem.at[1])
    load_v = pltpu.make_async_copy(values_ref, v_ref.at[:, pl.ds(0, size)], local_sem.at[2])
    load_new.start()
    load_k.start()
    load_q.start()
    load_v.start()
    for load in small:
        load.start()

    barrier = pltpu.get_barrier_semaphore()
    for steps in range(1, layers):
        pl.semaphore_signal(barrier, inc=1, device_id={"ctx": along_z(steps)}, device_id_type=MESH)
    pl.semaphore_signal(barrier, inc=1, device_id={"ctx": pair}, device_id_type=MESH)
    for steps in range(1, heads_axis):
        pl.semaphore_signal(
            barrier, inc=1, device_id={"head": along_head(steps)}, device_id_type=MESH
        )

    out_row = lax.broadcasted_iota(jnp.int32, (2 * new_tok, 2 * new_tok), 0)
    in_row = lax.broadcasted_iota(jnp.int32, (2 * new_tok, 2 * new_tok), 1)
    wanted = jnp.where(out_row < new_tok, 2 * out_row, 2 * (out_row - new_tok) + 1)
    order = jnp.where(in_row == wanted, 1.0, 0.0).astype(jnp.bfloat16)
    load_new.wait()
    all_new[z, x, head] = jnp.dot(
        order, new_ref[...], preferred_element_type=jnp.float32
    ).astype(jnp.bfloat16)
    v_ref[:, pl.ds(size, size)] = jnp.ones((store_rows, size), jnp.bfloat16)

    pl.semaphore_wait(barrier, layers + heads_axis - 1)

    def remote(src, dst, send_sem, recv_sem, device):
        return pltpu.make_async_remote_copy(
            src_ref=src,
            dst_ref=dst,
            send_sem=send_sem,
            recv_sem=recv_sem,
            device_id=device,
            device_id_type=MESH,
        )

    def send_q(steps):
        slot = layers - steps
        return remote(
            queries_ref,
            qz_ref.at[slot],
            qz_send.at[steps],
            qz_recv.at[slot],
            {"ctx": along_z(steps)},
        )

    def take_q(slot):
        return remote(
            queries_ref, qz_ref.at[slot], qz_send.at[slot], qz_recv.at[slot], {"ctx": along_z(slot)}
        )

    def pass_q(slot):
        return remote(
            qz_ref.at[slot], qx_ref.at[slot], qx_send.at[slot], qx_recv.at[slot], {"ctx": pair}
        )

    first_pass = remote(
        queries_ref, qx_ref.at[0], qx_send.at[0], qx_recv.at[0], {"ctx": pair}
    )

    def cross(slot):
        return (
            remote(sx_o.at[slot], rx_o.at[slot], xo_send.at[slot], xo_recv.at[slot], {"ctx": pair}),
            remote(sx_l.at[slot], rx_l.at[slot], xl_send.at[slot], xl_recv.at[slot], {"ctx": pair}),
        )

    def give_back(steps):
        slot = layers - steps
        device = {"ctx": along_z(steps)}
        return (
            remote(sz_o.at[steps], rz_o.at[slot], zo_send.at[steps], zo_recv.at[slot], device),
            remote(sz_l.at[steps], rz_l.at[slot], zl_send.at[steps], zl_recv.at[slot], device),
        )

    def get_back(slot):
        device = {"ctx": along_z(slot)}
        return (
            remote(sz_o.at[slot], rz_o.at[slot], zo_send.at[slot], zo_recv.at[slot], device),
            remote(sz_l.at[slot], rz_l.at[slot], zl_send.at[slot], zl_recv.at[slot], device),
        )

    def new_z(steps):
        mine = all_new.at[z, x, head]
        return remote(
            mine, mine, nz_send.at[steps], nz_recv.at[layers - steps], {"ctx": along_z(steps)}
        )

    def new_z_taken(slot):
        theirs = all_new.at[lax.rem(z + slot, layers), x, head]
        return remote(theirs, theirs, nz_send.at[slot], nz_recv.at[slot], {"ctx": along_z(slot)})

    def new_x(parity):
        block = all_new.at[:, parity, head]
        return remote(block, block, nx_send, nx_recv, {"ctx": pair})

    def new_h(steps):
        mine = all_new.at[:, :, head]
        return remote(
            mine,
            mine,
            nh_send.at[steps],
            nh_recv.at[heads_axis - steps],
            {"head": along_head(steps)},
        )

    def new_h_taken(slot):
        theirs = all_new.at[:, :, along_head(slot)]
        return remote(
            theirs, theirs, nh_send.at[slot], nh_recv.at[slot], {"head": along_head(slot)}
        )

    first_pass.start()
    for steps in range(1, layers):
        send_q(steps).start()
    for steps in range(1, layers):
        new_z(steps).start()

    for load in small:
        load.wait()
    dead = []
    for number in range(slots):
        live = jnp.int32(0)
        for place in range(slots):
            hit = (table_ref[0, place] == number) & (place < count_ref[0])
            live = jnp.where(hit, jnp.int32(1), live)
        dead.append(jnp.where(live == 1, jnp.float32(0.0), jnp.float32(FAR)))

    def partial(query_rows):
        scores, top = [], None
        for number in range(slots):
            found = jnp.dot(
                query_rows,
                kt_ref[:, pl.ds(number * page, page)],
                preferred_element_type=jnp.float32,
            )
            scores.append(found)
            page_top = jnp.max(found, axis=1, keepdims=True) - dead[number]
            top = page_top if top is None else jnp.maximum(top, page_top)
        summed = None
        for number in range(slots):
            weights = jnp.exp2((scores[number] - (top + dead[number])) * scale)
            product = jnp.dot(
                weights.astype(jnp.bfloat16),
                v_ref[pl.ds(number * page, page), :],
                preferred_element_type=jnp.float32,
            )
            summed = product if summed is None else summed + product
        totals = summed[:, size:]
        level = top * scale + jnp.log2(totals)
        return summed[:, :size] / totals, level

    def write(mean, level, mean_ref, level_ref):
        largest = jnp.max(jnp.abs(mean), axis=1, keepdims=True)
        steps = jnp.round(mean * (STEPS / jnp.maximum(largest, TINY)))
        mean_ref[...] = steps.astype(jnp.int32).astype(jnp.int16)
        lane = lax.broadcasted_iota(jnp.int32, (rows, size), 1)
        level_ref[...] = jnp.where(lane == 0, level, largest * (1.0 / STEPS)).T[:8, :]

    def read(mean_ref, level_ref):
        level = jnp.broadcast_to(level_ref[0:1, :], (size, rows)).T
        step = jnp.broadcast_to(level_ref[1:2, :], (size, rows)).T
        return mean_ref[...].astype(jnp.int32).astype(jnp.float32) * step, level

    def merged(parts):
        top = functools.reduce(jnp.maximum, [level for _, level in parts])
        share = [jnp.exp2(level - top) for _, level in parts]
        whole = functools.reduce(jnp.add, share)
        summed = functools.reduce(jnp.add, [one * mean for one, (mean, _) in zip(share, parts)])
        return summed / whole, top + jnp.log2(whole)

    def join_pair(slot):
        for copy in cross(slot):
            copy.wait_recv()
        return merged(
            [
                (own_o[slot], own_l[slot]),
                read(rx_o.at[slot], rx_l.at[slot]),
            ]
        )

    def send_joined(slot):
        mean, level = join_pair(slot)
        write(mean, level, sz_o.at[slot], sz_l.at[slot])
        for copy in give_back(slot):
            copy.start()

    def serve_pair(slot):
        mean, level = partial(qx_ref[slot])
        write(mean, level, sx_o.at[slot], sx_l.at[slot])
        for copy in cross(slot):
            copy.start()

    load_k.wait()
    kt_ref[...] = k_ref[...].T
    load_q.wait()
    load_v.wait()
    mean, level = partial(qz_ref[0])
    own_o[0] = mean
    own_l[0] = level
    take_q(1).wait_recv()
    pass_q(1).start()

    def layer_step(slot, carry):
        mean, level = partial(qz_ref[slot])
        own_o[slot] = mean
        own_l[slot] = level

        @pl.when(slot < layers - 1)
        def _():
            take_q(slot + 1).wait_recv()
            pass_q(slot + 1).start()

        pass_q(slot).wait_recv()
        serve_pair(slot)

        @pl.when(slot == 1)
        def _():
            for other in range(1, layers):
                new_z_taken(other).wait_recv()
            new_x(x).start()

        @pl.when(slot >= 2)
        def _():
            send_joined(slot - 1)

        @pl.when(slot == 2)
        def _():
            new_x(1 - x).wait_recv()
            for steps in range(1, heads_axis):
                new_h(steps).start()

        return carry

    lax.fori_loop(1, layers, layer_step, 0)
    first_pass.wait_recv()
    serve_pair(0)
    send_joined(layers - 1)

    for slot in range(1, heads_axis):
        new_h_taken(slot).wait_recv()
    tokens = layers * 2 * heads_axis * new_tok
    gathered = all_new[...].astype(jnp.float32).reshape(tokens // new_tok, 2, new_tok, size)
    new_keys = gathered[:, 0].reshape(tokens, size).astype(jnp.bfloat16)
    new_values = gathered[:, 1].reshape(tokens, size).astype(jnp.bfloat16)

    mine = owner_ref[...] == store
    target = jnp.where(mine, 2 * offset_ref[...], -2)
    place = lax.broadcasted_iota(jnp.int32, (appended_ref.shape[0], tokens), 0)
    key_rows = jnp.where(place == target, 1.0, 0.0).astype(jnp.bfloat16)
    value_rows = jnp.where(place == target + 1, 1.0, 0.0).astype(jnp.bfloat16)
    appended_ref[...] = (
        jnp.dot(key_rows, new_keys, preferred_element_type=jnp.float32)
        + jnp.dot(value_rows, new_values, preferred_element_type=jnp.float32)
    ).astype(jnp.bfloat16)

    scores = lax.dot_general(qz_ref[0], new_keys, NT, preferred_element_type=jnp.float32)
    column = lax.broadcasted_iota(jnp.int32, (1, tokens), 1) * head_dev - store * rows
    row = lax.broadcasted_iota(jnp.int32, (rows, tokens), 0)
    scores = jnp.where(column <= row, scores, -FAR)
    top = jnp.max(scores, axis=1, keepdims=True)
    weights = jnp.exp2((scores - top) * scale)
    totals = jnp.sum(weights, axis=1, keepdims=True)
    summed = jnp.dot(weights.astype(jnp.bfloat16), new_values, preferred_element_type=jnp.float32)
    self_level = jnp.broadcast_to(top * scale + jnp.log2(totals), (rows, size))
    parts = [(summed / totals, self_level), join_pair(0)]
    for slot in range(1, layers):
        for copy in get_back(slot):
            copy.wait_recv()
        parts.append(read(rz_o.at[slot], rz_l.at[slot]))
    attended_ref[...] = merged(parts)[0].astype(jnp.bfloat16)

    first_pass.wait_send()
    for slot in range(layers):
        for copy in cross(slot):
            copy.wait_send()
        if slot:
            send_q(slot).wait_send()
            pass_q(slot).wait_send()
            new_z(slot).wait_send()
            for copy in give_back(slot):
                copy.wait_send()
    new_x(x).wait_send()
    for steps in range(1, heads_axis):
        new_h(steps).wait_send()


def shards(
    queries, cache_keys, cache_values, page_table, page_count, new_kv, new_owner, new_offset
):
    tok_dev, head_dev, size = queries.shape
    new_tok = new_kv.shape[0]
    slots = page_table.shape[1]
    store_rows = cache_keys.shape[0]
    stores = lax.axis_size("ctx")
    heads_axis = lax.axis_size("head")
    layers = stores // 2
    rows = tok_dev * head_dev
    append_rows = 2 * tok_dev
    tokens = new_owner.shape[0]
    bf16, f32 = jnp.bfloat16, jnp.float32
    vmem = pl.BlockSpec(memory_space=pltpu.VMEM)
    smem = pl.BlockSpec(memory_space=pltpu.SMEM)
    hbm = pl.BlockSpec(memory_space=pltpu.HBM)
    mean_block = pltpu.VMEM((layers, rows, size), bf16)
    part_block = pltpu.VMEM((layers, rows, size), jnp.int16)
    level_block = pltpu.VMEM((layers, 8, rows), f32)
    dma = pltpu.SemaphoreType.DMA((layers,))
    attended, appended = pl.pallas_call(
        functools.partial(attention_kernel, layers, heads_axis, head_dev, slots),
        out_shape=(
            jax.ShapeDtypeStruct((rows, size), bf16),
            jax.ShapeDtypeStruct((2 * append_rows, size), bf16),
        ),
        in_specs=[hbm, smem] + [hbm] * 6,
        out_specs=(vmem, vmem),
        scratch_shapes=[
            pltpu.SMEM((1, slots), jnp.int32),
            pltpu.VMEM((2 * new_tok, size), bf16),
            pltpu.VMEM((1, tokens), jnp.int32),
            pltpu.VMEM((1, tokens), jnp.int32),
            pltpu.VMEM((store_rows, size), bf16),
            pltpu.VMEM((size, store_rows), bf16),
            pltpu.VMEM((store_rows, 2 * size), bf16),
            mean_block,
            mean_block,
            pltpu.VMEM((layers, rows, size), f32),
            pltpu.VMEM((layers, rows, size), f32),
            part_block,
            level_block,
            part_block,
            level_block,
            part_block,
            level_block,
            part_block,
            level_block,
            pltpu.VMEM((layers, 2, heads_axis, 2 * new_tok, size), bf16),
            pltpu.SemaphoreType.DMA((7,)),
        ]
        + [dma] * 14
        + [
            pltpu.SemaphoreType.DMA,
            pltpu.SemaphoreType.DMA,
            pltpu.SemaphoreType.DMA((heads_axis,)),
            pltpu.SemaphoreType.DMA((heads_axis,)),
        ],
        compiler_params=pltpu.CompilerParams(
            collective_id=0, has_side_effects=True, vmem_limit_bytes=62 * 1024 * 1024
        ),
    )(
        page_table,
        page_count,
        queries.reshape(rows, size),
        cache_keys,
        cache_values,
        new_kv.reshape(2 * new_tok, size),
        new_owner.reshape(1, tokens),
        new_offset.reshape(1, tokens),
    )
    return (
        attended.reshape(tok_dev, head_dev, size),
        appended.reshape(append_rows, 2, size),
    )


def solution(mesh):
    in_specs = (
        P("ctx", "head", None),
        P("ctx", None),
        P("ctx", None),
        P("ctx", None),
        P("ctx"),
        P(("ctx", "head"), None, None),
        P(),
        P(),
    )
    out_specs = (P("ctx", "head", None), P("ctx", None, None))
    return jax.shard_map(shards, mesh=mesh, in_specs=in_specs, out_specs=out_specs, check_vma=False)
```

```python
import functools
import math

import jax
import jax.numpy as jnp
from jax import lax
from jax.experimental import pallas as pl
from jax.experimental.pallas import tpu as pltpu
from jax.sharding import PartitionSpec as P

MESH = pl.DeviceIdType.MESH
FAR = 1e30
STEPS = 32767.0
TINY = 1e-30


def attention_kernel(
    layers,
    heads_axis,
    head_dev,
    slots,
    table_hbm,
    count_ref,
    queries_ref,
    keys_ref,
    values_ref,
    new_hbm,
    owner_hbm,
    offset_hbm,
    attended_ref,
    appended_ref,
    table_ref,
    new_ref,
    owner_ref,
    offset_ref,
    q_ref,
    k_ref,
    v_ref,
    vt_ref,
    qz_ref,
    qx_ref,
    own_o,
    own_l,
    sx_o,
    sx_l,
    rx_o,
    rx_l,
    sz_o,
    sz_l,
    rz_o,
    rz_l,
    all_new,
    local_sem,
    qz_send,
    qz_recv,
    qx_send,
    qx_recv,
    xo_send,
    xo_recv,
    xl_send,
    xl_recv,
    zo_send,
    zo_recv,
    zl_send,
    zl_recv,
    nz_send,
    nz_recv,
    nx_send,
    nx_recv,
    nh_send,
    nh_recv,
):
    rows, size = queries_ref.shape
    store_rows = keys_ref.shape[0]
    page = store_rows // slots
    new_tok = new_hbm.shape[0] // 2
    scale = math.log2(math.e) / math.sqrt(size)
    store = lax.axis_index("ctx")
    head = lax.axis_index("head")
    z = lax.div(store, 2)
    x = lax.rem(store, 2)
    pair = store + 1 - 2 * x

    def along_z(steps):
        return 2 * lax.rem(z + steps, layers) + x

    def along_head(steps):
        return lax.rem(head + steps, heads_axis)

    load_new = pltpu.make_async_copy(new_hbm, new_ref, local_sem.at[3])
    small = [
        pltpu.make_async_copy(table_hbm, table_ref, local_sem.at[4]),
        pltpu.make_async_copy(owner_hbm, owner_ref, local_sem.at[5]),
        pltpu.make_async_copy(offset_hbm, offset_ref, local_sem.at[6]),
    ]
    load_q = pltpu.make_async_copy(queries_ref, q_ref, local_sem.at[0])
    load_k = pltpu.make_async_copy(keys_ref, k_ref, local_sem.at[1])
    load_v = pltpu.make_async_copy(values_ref, v_ref, local_sem.at[2])
    load_q.start()
    load_new.start()
    load_k.start()
    load_v.start()
    for load in small:
        load.start()

    barrier = pltpu.get_barrier_semaphore()
    for steps in range(1, layers):
        pl.semaphore_signal(barrier, inc=1, device_id={"ctx": along_z(steps)}, device_id_type=MESH)
    pl.semaphore_signal(barrier, inc=1, device_id={"ctx": pair}, device_id_type=MESH)
    for steps in range(1, heads_axis):
        pl.semaphore_signal(
            barrier, inc=1, device_id={"head": along_head(steps)}, device_id_type=MESH
        )

    out_row = lax.broadcasted_iota(jnp.int32, (2 * new_tok, 2 * new_tok), 0)
    in_row = lax.broadcasted_iota(jnp.int32, (2 * new_tok, 2 * new_tok), 1)
    wanted = jnp.where(out_row < new_tok, 2 * out_row, 2 * (out_row - new_tok) + 1)
    order = jnp.where(in_row == wanted, 1.0, 0.0).astype(jnp.bfloat16)
    load_new.wait()
    all_new[z, x, head] = jnp.dot(
        order, new_ref[...], preferred_element_type=jnp.float32
    ).astype(jnp.bfloat16)
    load_q.wait()
    qz_ref[0] = q_ref[...].T

    pl.semaphore_wait(barrier, layers + heads_axis - 1)

    def remote(src, dst, send_sem, recv_sem, device):
        return pltpu.make_async_remote_copy(
            src_ref=src,
            dst_ref=dst,
            send_sem=send_sem,
            recv_sem=recv_sem,
            device_id=device,
            device_id_type=MESH,
        )

    def send_q(steps):
        slot = layers - steps
        return remote(
            qz_ref.at[0],
            qz_ref.at[slot],
            qz_send.at[steps],
            qz_recv.at[slot],
            {"ctx": along_z(steps)},
        )

    def take_q(slot):
        return remote(
            qz_ref.at[0], qz_ref.at[slot], qz_send.at[slot], qz_recv.at[slot], {"ctx": along_z(slot)}
        )

    def pass_q(slot):
        return remote(
            qz_ref.at[slot], qx_ref.at[slot], qx_send.at[slot], qx_recv.at[slot], {"ctx": pair}
        )

    first_pass = remote(
        qz_ref.at[0], qx_ref.at[0], qx_send.at[0], qx_recv.at[0], {"ctx": pair}
    )

    def cross(slot):
        return (
            remote(sx_o.at[slot], rx_o.at[slot], xo_send.at[slot], xo_recv.at[slot], {"ctx": pair}),
            remote(sx_l.at[slot], rx_l.at[slot], xl_send.at[slot], xl_recv.at[slot], {"ctx": pair}),
        )

    def give_back(steps):
        slot = layers - steps
        device = {"ctx": along_z(steps)}
        return (
            remote(sz_o.at[steps], rz_o.at[slot], zo_send.at[steps], zo_recv.at[slot], device),
            remote(sz_l.at[steps], rz_l.at[slot], zl_send.at[steps], zl_recv.at[slot], device),
        )

    def get_back(slot):
        device = {"ctx": along_z(slot)}
        return (
            remote(sz_o.at[slot], rz_o.at[slot], zo_send.at[slot], zo_recv.at[slot], device),
            remote(sz_l.at[slot], rz_l.at[slot], zl_send.at[slot], zl_recv.at[slot], device),
        )

    def new_z(steps):
        mine = all_new.at[z, x, head]
        return remote(
            mine, mine, nz_send.at[steps], nz_recv.at[layers - steps], {"ctx": along_z(steps)}
        )

    def new_z_taken(slot):
        theirs = all_new.at[lax.rem(z + slot, layers), x, head]
        return remote(theirs, theirs, nz_send.at[slot], nz_recv.at[slot], {"ctx": along_z(slot)})

    def new_x(parity):
        block = all_new.at[:, parity, head]
        return remote(block, block, nx_send, nx_recv, {"ctx": pair})

    def new_h(steps):
        mine = all_new.at[:, :, head]
        return remote(
            mine,
            mine,
            nh_send.at[steps],
            nh_recv.at[heads_axis - steps],
            {"head": along_head(steps)},
        )

    def new_h_taken(slot):
        theirs = all_new.at[:, :, along_head(slot)]
        return remote(
            theirs, theirs, nh_send.at[slot], nh_recv.at[slot], {"head": along_head(slot)}
        )

    first_pass.start()
    for steps in range(1, layers):
        send_q(steps).start()
    for steps in range(1, layers):
        new_z(steps).start()

    for load in small:
        load.wait()
    dead = []
    for number in range(slots):
        live = jnp.int32(0)
        for place in range(slots):
            hit = (table_ref[0, place] == number) & (place < count_ref[0])
            live = jnp.where(hit, jnp.int32(1), live)
        dead.append(jnp.where(live == 1, jnp.float32(0.0), jnp.float32(FAR)))

    def partial(query_columns):
        scores, top = [], None
        for number in range(slots):
            found = jnp.dot(
                k_ref[pl.ds(number * page, page), :],
                query_columns,
                preferred_element_type=jnp.float32,
            )
            scores.append(found)
            page_top = jnp.max(found, axis=0, keepdims=True) - dead[number]
            top = page_top if top is None else jnp.maximum(top, page_top)
        summed = None
        for number in range(slots):
            weights = jnp.exp2((scores[number] - (top + dead[number])) * scale)
            product = jnp.dot(
                vt_ref[:, pl.ds(number * page, page)],
                weights.astype(jnp.bfloat16),
                preferred_element_type=jnp.float32,
            )
            summed = product if summed is None else summed + product
        totals = summed[size : size + 1, :]
        return summed[:size, :] / totals, top * scale + jnp.log2(totals)

    def write(mean, level, mean_ref, level_ref):
        largest = jnp.max(jnp.abs(mean), axis=0, keepdims=True)
        steps = jnp.round(mean * (STEPS / jnp.maximum(largest, TINY)))
        mean_ref[...] = steps.astype(jnp.int32).astype(jnp.int16)
        line = lax.broadcasted_iota(jnp.int32, (8, rows), 0)
        level_ref[...] = jnp.where(line == 0, level, largest * (1.0 / STEPS))

    def read(mean_ref, level_ref):
        step = level_ref[1:2, :]
        return mean_ref[...].astype(jnp.int32).astype(jnp.float32) * step, level_ref[0:1, :]

    def merged(parts):
        top = functools.reduce(jnp.maximum, [level for _, level in parts])
        share = [jnp.exp2(level - top) for _, level in parts]
        whole = functools.reduce(jnp.add, share)
        summed = functools.reduce(jnp.add, [one * mean for one, (mean, _) in zip(share, parts)])
        return summed / whole, top + jnp.log2(whole)

    def join_pair(slot):
        for copy in cross(slot):
            copy.wait_recv()
        return merged(
            [
                (own_o[slot], own_l[slot, 0:1, :]),
                read(rx_o.at[slot], rx_l.at[slot]),
            ]
        )

    def send_joined(slot):
        mean, level = join_pair(slot)
        write(mean, level, sz_o.at[slot], sz_l.at[slot])
        for copy in give_back(slot):
            copy.start()

    def serve_pair(slot):
        mean, level = partial(qx_ref[slot])
        write(mean, level, sx_o.at[slot], sx_l.at[slot])
        for copy in cross(slot):
            copy.start()

    load_k.wait()
    load_v.wait()
    vt_ref[pl.ds(0, size), :] = v_ref[...].T
    vt_ref[pl.ds(size, 16), :] = jnp.ones((16, store_rows), jnp.bfloat16)
    mean, level = partial(qz_ref[0])
    own_o[0] = mean
    own_l[0, 0:1, :] = level
    take_q(1).wait_recv()
    pass_q(1).start()

    def layer_step(slot, carry):
        mean, level = partial(qz_ref[slot])
        own_o[slot] = mean
        own_l[slot, 0:1, :] = level

        @pl.when(slot < layers - 1)
        def _():
            take_q(slot + 1).wait_recv()
            pass_q(slot + 1).start()

        pass_q(slot).wait_recv()
        serve_pair(slot)

        @pl.when(slot == 1)
        def _():
            for other in range(1, layers):
                new_z_taken(other).wait_recv()
            new_x(x).start()

        @pl.when(slot >= 2)
        def _():
            send_joined(slot - 1)

        @pl.when(slot == 2)
        def _():
            new_x(1 - x).wait_recv()
            for steps in range(1, heads_axis):
                new_h(steps).start()

        return carry

    lax.fori_loop(1, layers, layer_step, 0)
    first_pass.wait_recv()
    serve_pair(0)
    send_joined(layers - 1)

    for slot in range(1, heads_axis):
        new_h_taken(slot).wait_recv()
    tokens = layers * 2 * heads_axis * new_tok
    gathered = all_new[...].astype(jnp.float32).reshape(tokens // new_tok, 2, new_tok, size)
    new_keys = gathered[:, 0].reshape(tokens, size).astype(jnp.bfloat16)
    new_values = gathered[:, 1].reshape(tokens, size).astype(jnp.bfloat16)

    mine = owner_ref[...] == store
    target = jnp.where(mine, 2 * offset_ref[...], -2)
    place = lax.broadcasted_iota(jnp.int32, (appended_ref.shape[0], tokens), 0)
    key_rows = jnp.where(place == target, 1.0, 0.0).astype(jnp.bfloat16)
    value_rows = jnp.where(place == target + 1, 1.0, 0.0).astype(jnp.bfloat16)
    appended_ref[...] = (
        jnp.dot(key_rows, new_keys, preferred_element_type=jnp.float32)
        + jnp.dot(value_rows, new_values, preferred_element_type=jnp.float32)
    ).astype(jnp.bfloat16)

    scores = jnp.dot(new_keys, qz_ref[0], preferred_element_type=jnp.float32)
    token = lax.broadcasted_iota(jnp.int32, (tokens, rows), 0)
    asker = lax.broadcasted_iota(jnp.int32, (tokens, rows), 1)
    scores = jnp.where(token * head_dev - store * rows <= asker, scores, -FAR)
    top = jnp.max(scores, axis=0, keepdims=True)
    weights = jnp.exp2((scores - top) * scale)
    totals = jnp.sum(weights, axis=0, keepdims=True)
    summed = jnp.dot(
        new_values.T, weights.astype(jnp.bfloat16), preferred_element_type=jnp.float32
    )
    parts = [(summed / totals, top * scale + jnp.log2(totals)), join_pair(0)]
    for slot in range(1, layers):
        for copy in get_back(slot):
            copy.wait_recv()
        parts.append(read(rz_o.at[slot], rz_l.at[slot]))
    attended_ref[...] = merged(parts)[0].T.astype(jnp.bfloat16)

    first_pass.wait_send()
    for slot in range(layers):
        for copy in cross(slot):
            copy.wait_send()
        if slot:
            send_q(slot).wait_send()
            pass_q(slot).wait_send()
            new_z(slot).wait_send()
            for copy in give_back(slot):
                copy.wait_send()
    new_x(x).wait_send()
    for steps in range(1, heads_axis):
        new_h(steps).wait_send()


def shards(
    queries, cache_keys, cache_values, page_table, page_count, new_kv, new_owner, new_offset
):
    tok_dev, head_dev, size = queries.shape
    new_tok = new_kv.shape[0]
    slots = page_table.shape[1]
    store_rows = cache_keys.shape[0]
    stores = lax.axis_size("ctx")
    heads_axis = lax.axis_size("head")
    layers = stores // 2
    rows = tok_dev * head_dev
    append_rows = 2 * tok_dev
    tokens = new_owner.shape[0]
    bf16, f32 = jnp.bfloat16, jnp.float32
    vmem = pl.BlockSpec(memory_space=pltpu.VMEM)
    smem = pl.BlockSpec(memory_space=pltpu.SMEM)
    hbm = pl.BlockSpec(memory_space=pltpu.HBM)
    mean_block = pltpu.VMEM((layers, size, rows), bf16)
    part_block = pltpu.VMEM((layers, size, rows), jnp.int16)
    level_block = pltpu.VMEM((layers, 8, rows), f32)
    dma = pltpu.SemaphoreType.DMA((layers,))
    attended, appended = pl.pallas_call(
        functools.partial(attention_kernel, layers, heads_axis, head_dev, slots),
        out_shape=(
            jax.ShapeDtypeStruct((rows, size), bf16),
            jax.ShapeDtypeStruct((2 * append_rows, size), bf16),
        ),
        in_specs=[hbm, smem] + [hbm] * 6,
        out_specs=(vmem, vmem),
        scratch_shapes=[
            pltpu.SMEM((1, slots), jnp.int32),
            pltpu.VMEM((2 * new_tok, size), bf16),
            pltpu.VMEM((1, tokens), jnp.int32),
            pltpu.VMEM((1, tokens), jnp.int32),
            pltpu.VMEM((rows, size), bf16),
            pltpu.VMEM((store_rows, size), bf16),
            pltpu.VMEM((store_rows, size), bf16),
            pltpu.VMEM((size + 16, store_rows), bf16),
            mean_block,
            mean_block,
            pltpu.VMEM((layers, size, rows), f32),
            level_block,
            part_block,
            level_block,
            part_block,
            level_block,
            part_block,
            level_block,
            part_block,
            level_block,
            pltpu.VMEM((layers, 2, heads_axis, 2 * new_tok, size), bf16),
            pltpu.SemaphoreType.DMA((7,)),
        ]
        + [dma] * 14
        + [
            pltpu.SemaphoreType.DMA,
            pltpu.SemaphoreType.DMA,
            pltpu.SemaphoreType.DMA((heads_axis,)),
            pltpu.SemaphoreType.DMA((heads_axis,)),
        ],
        compiler_params=pltpu.CompilerParams(
            collective_id=0, has_side_effects=True, vmem_limit_bytes=62 * 1024 * 1024
        ),
    )(
        page_table,
        page_count,
        queries.reshape(rows, size),
        cache_keys,
        cache_values,
        new_kv.reshape(2 * new_tok, size),
        new_owner.reshape(1, tokens),
        new_offset.reshape(1, tokens),
    )
    return (
        attended.reshape(tok_dev, head_dev, size),
        appended.reshape(append_rows, 2, size),
    )


def solution(mesh):
    in_specs = (
        P("ctx", "head", None),
        P("ctx", None),
        P("ctx", None),
        P("ctx", None),
        P("ctx"),
        P(("ctx", "head"), None, None),
        P(),
        P(),
    )
    out_specs = (P("ctx", "head", None), P("ctx", None, None))
    return jax.shard_map(shards, mesh=mesh, in_specs=in_specs, out_specs=out_specs, check_vma=False)
```

```python
import functools
import math

import jax
import jax.numpy as jnp
from jax import lax
from jax.experimental import pallas as pl
from jax.experimental.pallas import tpu as pltpu
from jax.sharding import PartitionSpec as P

MESH = pl.DeviceIdType.MESH
FAR = 1e30
STEPS = 32767.0
TINY = 1e-30


def attention_kernel(
    layers,
    heads_axis,
    head_dev,
    slots,
    table_hbm,
    count_ref,
    queries_ref,
    keys_ref,
    values_ref,
    new_hbm,
    owner_hbm,
    offset_hbm,
    attended_ref,
    appended_ref,
    table_ref,
    new_ref,
    owner_ref,
    offset_ref,
    q_ref,
    v_ref,
    near_k,
    near_v,
    far_k,
    far_v,
    near_dead,
    far_dead,
    qz_ref,
    own_o,
    own_l,
    sz_o,
    sz_l,
    rz_o,
    rz_l,
    all_new,
    local_sem,
    qz_send,
    qz_recv,
    xk_send,
    xk_recv,
    xv_send,
    xv_recv,
    xd_send,
    xd_recv,
    yk_send,
    yk_recv,
    yv_send,
    yv_recv,
    ck_send,
    ck_recv,
    cv_send,
    cv_recv,
    zo_send,
    zo_recv,
    zl_send,
    zl_recv,
    nz_send,
    nz_recv,
    nx_send,
    nx_recv,
    nh_send,
    nh_recv,
):
    rows, size = queries_ref.shape
    chunk = keys_ref.shape[1]
    chunks_page = heads_axis // slots
    chips = heads_axis // 2
    new_tok = new_hbm.shape[0] // 2
    scale = math.log2(math.e) / math.sqrt(size)
    store = lax.axis_index("ctx")
    head = lax.axis_index("head")
    z = lax.div(store, 2)
    x = lax.rem(store, 2)
    pair = store + 1 - 2 * x
    core = lax.rem(head, 2)
    other_core = head + 1 - 2 * core

    def along_z(steps):
        return 2 * lax.rem(z + steps, layers) + x

    def along_head(steps):
        return lax.rem(head + steps, heads_axis)

    load_new = pltpu.make_async_copy(new_hbm, new_ref, local_sem.at[3])
    small = [
        pltpu.make_async_copy(table_hbm, table_ref, local_sem.at[4]),
        pltpu.make_async_copy(owner_hbm, owner_ref, local_sem.at[5]),
        pltpu.make_async_copy(offset_hbm, offset_ref, local_sem.at[6]),
    ]
    load_q = pltpu.make_async_copy(queries_ref, q_ref, local_sem.at[0])
    load_k = pltpu.make_async_copy(keys_ref, near_k, local_sem.at[1])
    load_v = pltpu.make_async_copy(values_ref, v_ref, local_sem.at[2])
    load_q.start()
    load_new.start()
    load_k.start()
    load_v.start()
    for load in small:
        load.start()

    barrier = pltpu.get_barrier_semaphore()
    for steps in range(1, layers):
        pl.semaphore_signal(barrier, inc=1, device_id={"ctx": along_z(steps)}, device_id_type=MESH)
    pl.semaphore_signal(barrier, inc=1, device_id={"ctx": pair}, device_id_type=MESH)
    for steps in range(1, heads_axis):
        pl.semaphore_signal(
            barrier, inc=1, device_id={"head": along_head(steps)}, device_id_type=MESH
        )

    out_row = lax.broadcasted_iota(jnp.int32, (2 * new_tok, 2 * new_tok), 0)
    in_row = lax.broadcasted_iota(jnp.int32, (2 * new_tok, 2 * new_tok), 1)
    wanted = jnp.where(out_row < new_tok, 2 * out_row, 2 * (out_row - new_tok) + 1)
    order = jnp.where(in_row == wanted, 1.0, 0.0).astype(jnp.bfloat16)
    load_new.wait()
    all_new[z, x, head] = jnp.dot(
        order, new_ref[...], preferred_element_type=jnp.float32
    ).astype(jnp.bfloat16)
    load_q.wait()
    qz_ref[0] = q_ref[...].T
    for part in range(heads_axis):
        near_v[part, pl.ds(size, 16), :] = jnp.ones((16, chunk), jnp.bfloat16)
        far_v[part, pl.ds(size, 16), :] = jnp.ones((16, chunk), jnp.bfloat16)
    for load in small:
        load.wait()
    for number in range(slots):
        live = jnp.int32(0)
        for place in range(slots):
            hit = (table_ref[0, place] == number) & (place < count_ref[0])
            live = jnp.where(hit, jnp.int32(1), live)
        gap = jnp.where(live == 1, jnp.float32(0.0), jnp.float32(FAR))
        near_dead[pl.ds(8 * number, 8), :] = jnp.full((8, rows), gap, jnp.float32)
    load_k.wait()

    pl.semaphore_wait(barrier, layers + heads_axis - 1)

    def remote(src, dst, send_sem, recv_sem, device):
        return pltpu.make_async_remote_copy(
            src_ref=src,
            dst_ref=dst,
            send_sem=send_sem,
            recv_sem=recv_sem,
            device_id=device,
            device_id_type=MESH,
        )

    def send_q(steps):
        slot = layers - steps
        return remote(
            qz_ref.at[0],
            qz_ref.at[slot],
            qz_send.at[steps],
            qz_recv.at[slot],
            {"ctx": along_z(steps)},
        )

    def take_q(slot):
        return remote(
            qz_ref.at[0], qz_ref.at[slot], qz_send.at[slot], qz_recv.at[slot], {"ctx": along_z(slot)}
        )

    keys_over = remote(near_k.at[head], far_k.at[head], xk_send, xk_recv, {"ctx": pair})
    values_over = remote(
        near_v.at[head, pl.ds(0, size)],
        far_v.at[head, pl.ds(0, size)],
        xv_send,
        xv_recv,
        {"ctx": pair},
    )
    dead_over = remote(near_dead, far_dead, xd_send, xd_recv, {"ctx": pair})

    def far_part(buffer, owner, steps):
        part = lax.rem(owner + 2 * steps, heads_axis)
        return buffer.at[part, pl.ds(0, buffer.shape[1] - (16 if buffer is far_v else 0))]

    def to_chip(buffer, send_sem, recv_sem, steps):
        mine = far_part(buffer, head, 0)
        device = {"head": along_head(2 * steps)}
        return remote(mine, mine, send_sem.at[steps], recv_sem.at[chips - steps], device)

    def from_chip(buffer, send_sem, recv_sem, steps):
        theirs = far_part(buffer, head, steps)
        device = {"head": along_head(2 * steps)}
        return remote(theirs, theirs, send_sem.at[steps], recv_sem.at[steps], device)

    def to_core(buffer, send_sem, recv_sem, steps):
        mine = far_part(buffer, head, steps)
        device = {"head": other_core}
        return remote(mine, mine, send_sem.at[steps], recv_sem.at[steps], device)

    def from_core(buffer, send_sem, recv_sem, steps):
        theirs = far_part(buffer, other_core, steps)
        device = {"head": other_core}
        return remote(theirs, theirs, send_sem.at[steps], recv_sem.at[steps], device)

    def spread(over, buffer, chip_sems, core_sems):
        over.wait_recv()
        for steps in range(1, chips):
            to_chip(buffer, *chip_sems, steps).start()
        to_core(buffer, *core_sems, 0).start()

    def spread_on(buffer, chip_sems, core_sems):
        for steps in range(1, chips):
            from_chip(buffer, *chip_sems, steps).wait_recv()
            to_core(buffer, *core_sems, steps).start()

    key_sems = ((yk_send, yk_recv), (ck_send, ck_recv))
    value_sems = ((yv_send, yv_recv), (cv_send, cv_recv))

    def give_back(steps):
        slot = layers - steps
        device = {"ctx": along_z(steps)}
        return (
            remote(sz_o.at[steps], rz_o.at[slot], zo_send.at[steps], zo_recv.at[slot], device),
            remote(sz_l.at[steps], rz_l.at[slot], zl_send.at[steps], zl_recv.at[slot], device),
        )

    def get_back(slot):
        device = {"ctx": along_z(slot)}
        return (
            remote(sz_o.at[slot], rz_o.at[slot], zo_send.at[slot], zo_recv.at[slot], device),
            remote(sz_l.at[slot], rz_l.at[slot], zl_send.at[slot], zl_recv.at[slot], device),
        )

    def new_z(steps):
        mine = all_new.at[z, x, head]
        return remote(
            mine, mine, nz_send.at[steps], nz_recv.at[layers - steps], {"ctx": along_z(steps)}
        )

    def new_z_taken(slot):
        theirs = all_new.at[lax.rem(z + slot, layers), x, head]
        return remote(theirs, theirs, nz_send.at[slot], nz_recv.at[slot], {"ctx": along_z(slot)})

    def new_x(parity):
        block = all_new.at[:, parity, head]
        return remote(block, block, nx_send, nx_recv, {"ctx": pair})

    def new_h(steps):
        mine = all_new.at[:, :, head]
        return remote(
            mine,
            mine,
            nh_send.at[steps],
            nh_recv.at[heads_axis - steps],
            {"head": along_head(steps)},
        )

    def new_h_taken(slot):
        theirs = all_new.at[:, :, along_head(slot)]
        return remote(
            theirs, theirs, nh_send.at[slot], nh_recv.at[slot], {"head": along_head(slot)}
        )

    keys_over.start()
    for steps in range(1, layers):
        send_q(steps).start()
    load_v.wait()
    near_v[head, pl.ds(0, size), :] = v_ref[head].T
    values_over.start()
    dead_over.start()
    for steps in range(1, layers):
        new_z(steps).start()

    def partial(query_columns, keys, values, gaps):
        scores, top, dead = [], None, []
        for number in range(heads_axis):
            found = jnp.dot(keys[number], query_columns, preferred_element_type=jnp.float32)
            scores.append(found)
            dead.append(gaps[pl.ds(8 * (number // chunks_page), 1), :])
            page_top = jnp.max(found, axis=0, keepdims=True) - dead[number]
            top = page_top if top is None else jnp.maximum(top, page_top)
        summed = None
        for number in range(heads_axis):
            weights = jnp.exp2((scores[number] - (top + dead[number])) * scale)
            product = jnp.dot(
                values[number],
                weights.astype(jnp.bfloat16),
                preferred_element_type=jnp.float32,
            )
            summed = product if summed is None else summed + product
        totals = summed[size : size + 1, :]
        return summed[:size, :] / totals, top * scale + jnp.log2(totals)

    def write(mean, level, mean_ref, level_ref):
        largest = jnp.max(jnp.abs(mean), axis=0, keepdims=True)
        steps = jnp.round(mean * (STEPS / jnp.maximum(largest, TINY)))
        mean_ref[...] = steps.astype(jnp.int32).astype(jnp.int16)
        line = lax.broadcasted_iota(jnp.int32, (8, rows), 0)
        level_ref[...] = jnp.where(line == 0, level, largest * (1.0 / STEPS))

    def read(mean_ref, level_ref):
        step = level_ref[1:2, :]
        return mean_ref[...].astype(jnp.int32).astype(jnp.float32) * step, level_ref[0:1, :]

    def merged(parts):
        top = functools.reduce(jnp.maximum, [level for _, level in parts])
        share = [jnp.exp2(level - top) for _, level in parts]
        whole = functools.reduce(jnp.add, share)
        summed = functools.reduce(jnp.add, [one * mean for one, (mean, _) in zip(share, parts)])
        return summed / whole, top + jnp.log2(whole)

    def near_step(slot):
        mean, level = partial(qz_ref[slot], near_k, near_v, near_dead)
        own_o[slot] = mean
        own_l[slot, 0:1, :] = level

    def far_step(slot):
        found = partial(qz_ref[slot], far_k, far_v, far_dead)
        return merged([(own_o[slot], own_l[slot, 0:1, :]), found])

    for step in range(1, heads_axis):
        part = along_head(step)
        near_v[part, pl.ds(0, size), :] = v_ref[part].T
    near_step(0)
    spread(keys_over, far_k, *key_sems)

    def near_layer(slot, carry):
        take_q(slot).wait_recv()
        near_step(slot)

        @pl.when(slot == 1)
        def _():
            for other in range(1, layers):
                new_z_taken(other).wait_recv()
            new_x(x).start()

        @pl.when(slot == 2)
        def _():
            spread(values_over, far_v, *value_sems)

        return carry

    lax.fori_loop(1, layers, near_layer, 0)
    new_x(1 - x).wait_recv()
    for steps in range(1, heads_axis):
        new_h(steps).start()
    spread_on(far_k, *key_sems)
    spread_on(far_v, *value_sems)

    for slot in range(1, heads_axis):
        new_h_taken(slot).wait_recv()
    tokens = layers * 2 * heads_axis * new_tok
    gathered = all_new[...].astype(jnp.float32).reshape(tokens // new_tok, 2, new_tok, size)
    new_keys = gathered[:, 0].reshape(tokens, size).astype(jnp.bfloat16)
    new_values = gathered[:, 1].reshape(tokens, size).astype(jnp.bfloat16)

    mine = owner_ref[...] == store
    target = jnp.where(mine, 2 * offset_ref[...], -2)
    place = lax.broadcasted_iota(jnp.int32, (appended_ref.shape[0], tokens), 0)
    key_rows = jnp.where(place == target, 1.0, 0.0).astype(jnp.bfloat16)
    value_rows = jnp.where(place == target + 1, 1.0, 0.0).astype(jnp.bfloat16)
    appended_ref[...] = (
        jnp.dot(key_rows, new_keys, preferred_element_type=jnp.float32)
        + jnp.dot(value_rows, new_values, preferred_element_type=jnp.float32)
    ).astype(jnp.bfloat16)

    scores = jnp.dot(new_keys, qz_ref[0], preferred_element_type=jnp.float32)
    token = lax.broadcasted_iota(jnp.int32, (tokens, rows), 0)
    asker = lax.broadcasted_iota(jnp.int32, (tokens, rows), 1)
    scores = jnp.where(token * head_dev - store * rows <= asker, scores, -FAR)
    top = jnp.max(scores, axis=0, keepdims=True)
    weights = jnp.exp2((scores - top) * scale)
    totals = jnp.sum(weights, axis=0, keepdims=True)
    summed = jnp.dot(
        new_values.T, weights.astype(jnp.bfloat16), preferred_element_type=jnp.float32
    )
    parts = [(summed / totals, top * scale + jnp.log2(totals))]

    dead_over.wait_recv()
    for steps in range(chips):
        from_core(far_k, ck_send, ck_recv, steps).wait_recv()
        from_core(far_v, cv_send, cv_recv, steps).wait_recv()

    def far_layer(slot, carry):
        mean, level = far_step(slot)
        write(mean, level, sz_o.at[slot], sz_l.at[slot])
        for copy in give_back(slot):
            copy.start()
        return carry

    lax.fori_loop(1, layers, far_layer, 0)
    parts.append(far_step(0))
    for slot in range(1, layers):
        for copy in get_back(slot):
            copy.wait_recv()
        parts.append(read(rz_o.at[slot], rz_l.at[slot]))
    attended_ref[...] = merged(parts)[0].T.astype(jnp.bfloat16)

    for copy in (keys_over, values_over, dead_over):
        copy.wait_send()
    for steps in range(chips):
        if steps:
            to_chip(far_k, yk_send, yk_recv, steps).wait_send()
            to_chip(far_v, yv_send, yv_recv, steps).wait_send()
        to_core(far_k, ck_send, ck_recv, steps).wait_send()
        to_core(far_v, cv_send, cv_recv, steps).wait_send()
    for slot in range(1, layers):
        send_q(slot).wait_send()
        new_z(slot).wait_send()
        for copy in give_back(slot):
            copy.wait_send()
    new_x(x).wait_send()
    for steps in range(1, heads_axis):
        new_h(steps).wait_send()


def shards(
    queries, cache_keys, cache_values, page_table, page_count, new_kv, new_owner, new_offset
):
    tok_dev, head_dev, size = queries.shape
    new_tok = new_kv.shape[0]
    slots = page_table.shape[1]
    stores = lax.axis_size("ctx")
    heads_axis = lax.axis_size("head")
    layers = stores // 2
    chunk = cache_keys.shape[0] // heads_axis
    rows = tok_dev * head_dev
    append_rows = 2 * tok_dev
    tokens = new_owner.shape[0]
    bf16, f32 = jnp.bfloat16, jnp.float32
    vmem = pl.BlockSpec(memory_space=pltpu.VMEM)
    smem = pl.BlockSpec(memory_space=pltpu.SMEM)
    hbm = pl.BlockSpec(memory_space=pltpu.HBM)
    mean_block = pltpu.VMEM((layers, size, rows), bf16)
    part_block = pltpu.VMEM((layers, size, rows), jnp.int16)
    level_block = pltpu.VMEM((layers, 8, rows), f32)
    dma = pltpu.SemaphoreType.DMA((layers,))
    attended, appended = pl.pallas_call(
        functools.partial(attention_kernel, layers, heads_axis, head_dev, slots),
        out_shape=(
            jax.ShapeDtypeStruct((rows, size), bf16),
            jax.ShapeDtypeStruct((2 * append_rows, size), bf16),
        ),
        in_specs=[hbm, smem] + [hbm] * 6,
        out_specs=(vmem, vmem),
        scratch_shapes=[
            pltpu.SMEM((1, slots), jnp.int32),
            pltpu.VMEM((2 * new_tok, size), bf16),
            pltpu.VMEM((1, tokens), jnp.int32),
            pltpu.VMEM((1, tokens), jnp.int32),
            pltpu.VMEM((rows, size), bf16),
            pltpu.VMEM((heads_axis, chunk, size), bf16),
            pltpu.VMEM((heads_axis, chunk, size), bf16),
            pltpu.VMEM((heads_axis, size + 16, chunk), bf16),
            pltpu.VMEM((heads_axis, chunk, size), bf16),
            pltpu.VMEM((heads_axis, size + 16, chunk), bf16),
            pltpu.VMEM((8 * slots, rows), f32),
            pltpu.VMEM((8 * slots, rows), f32),
            mean_block,
            pltpu.VMEM((layers, size, rows), f32),
            level_block,
            part_block,
            level_block,
            part_block,
            level_block,
            pltpu.VMEM((layers, 2, heads_axis, 2 * new_tok, size), bf16),
            pltpu.SemaphoreType.DMA((7,)),
        ]
        + [dma] * 2
        + [pltpu.SemaphoreType.DMA] * 6
        + [pltpu.SemaphoreType.DMA((heads_axis // 2,))] * 8
        + [dma] * 6
        + [
            pltpu.SemaphoreType.DMA,
            pltpu.SemaphoreType.DMA,
            pltpu.SemaphoreType.DMA((heads_axis,)),
            pltpu.SemaphoreType.DMA((heads_axis,)),
        ],
        compiler_params=pltpu.CompilerParams(
            collective_id=0, has_side_effects=True, vmem_limit_bytes=62 * 1024 * 1024
        ),
    )(
        page_table,
        page_count,
        queries.reshape(rows, size),
        cache_keys.reshape(heads_axis, chunk, size),
        cache_values.reshape(heads_axis, chunk, size),
        new_kv.reshape(2 * new_tok, size),
        new_owner.reshape(1, tokens),
        new_offset.reshape(1, tokens),
    )
    return (
        attended.reshape(tok_dev, head_dev, size),
        appended.reshape(append_rows, 2, size),
    )


def solution(mesh):
    in_specs = (
        P("ctx", "head", None),
        P("ctx", None),
        P("ctx", None),
        P("ctx", None),
        P("ctx"),
        P(("ctx", "head"), None, None),
        P(),
        P(),
    )
    out_specs = (P("ctx", "head", None), P("ctx", None, None))
    return jax.shard_map(shards, mesh=mesh, in_specs=in_specs, out_specs=out_specs, check_vma=False)
```

```python
import functools
import math

import jax
import jax.numpy as jnp
from jax import lax
from jax.experimental import pallas as pl
from jax.experimental.pallas import tpu as pltpu
from jax.sharding import PartitionSpec as P

MESH = pl.DeviceIdType.MESH
FAR = 1e30
STEPS = 32767.0
TINY = 1e-30
PIECES = 4


def attention_kernel(
    layers,
    heads_axis,
    head_dev,
    slots,
    table_hbm,
    count_ref,
    queries_ref,
    keys_ref,
    values_ref,
    new_hbm,
    owner_hbm,
    offset_hbm,
    attended_ref,
    appended_ref,
    table_ref,
    new_ref,
    owner_ref,
    offset_ref,
    q_ref,
    v_ref,
    near_k,
    near_v,
    far_k,
    far_v,
    near_dead,
    far_dead,
    qz_ref,
    own_o,
    own_l,
    sz_o,
    sz_l,
    rz_o,
    rz_l,
    all_new,
    local_sem,
    qz_send,
    qz_recv,
    xk_send,
    xk_recv,
    xv_send,
    xv_recv,
    xd_send,
    xd_recv,
    yk_send,
    yk_recv,
    yv_send,
    yv_recv,
    ck_send,
    ck_recv,
    cv_send,
    cv_recv,
    zo_send,
    zo_recv,
    zl_send,
    zl_recv,
    nz_send,
    nz_recv,
    nx_send,
    nx_recv,
    nh_send,
    nh_recv,
):
    rows, size = queries_ref.shape
    chunk = keys_ref.shape[1]
    chunks_page = heads_axis // slots
    chips = heads_axis // 2
    new_tok = new_hbm.shape[0] // 2
    scale = math.log2(math.e) / math.sqrt(size)
    store = lax.axis_index("ctx")
    head = lax.axis_index("head")
    z = lax.div(store, 2)
    x = lax.rem(store, 2)
    pair = store + 1 - 2 * x
    core = lax.rem(head, 2)
    other_core = head + 1 - 2 * core

    def along_z(steps):
        return 2 * lax.rem(z + steps, layers) + x

    def along_head(steps):
        return lax.rem(head + steps, heads_axis)

    load_new = pltpu.make_async_copy(new_hbm, new_ref, local_sem.at[3])
    small = [
        pltpu.make_async_copy(table_hbm, table_ref, local_sem.at[4]),
        pltpu.make_async_copy(owner_hbm, owner_ref, local_sem.at[5]),
        pltpu.make_async_copy(offset_hbm, offset_ref, local_sem.at[6]),
    ]
    load_q = pltpu.make_async_copy(queries_ref, q_ref, local_sem.at[0])
    load_k = pltpu.make_async_copy(keys_ref, near_k, local_sem.at[1])
    load_v = pltpu.make_async_copy(values_ref, v_ref, local_sem.at[2])
    load_q.start()
    load_new.start()
    load_k.start()
    load_v.start()
    for load in small:
        load.start()

    barrier = pltpu.get_barrier_semaphore()
    for steps in range(1, layers):
        pl.semaphore_signal(barrier, inc=1, device_id={"ctx": along_z(steps)}, device_id_type=MESH)
    pl.semaphore_signal(barrier, inc=1, device_id={"ctx": pair}, device_id_type=MESH)
    for steps in range(1, heads_axis):
        pl.semaphore_signal(
            barrier, inc=1, device_id={"head": along_head(steps)}, device_id_type=MESH
        )

    out_row = lax.broadcasted_iota(jnp.int32, (2 * new_tok, 2 * new_tok), 0)
    in_row = lax.broadcasted_iota(jnp.int32, (2 * new_tok, 2 * new_tok), 1)
    wanted = jnp.where(out_row < new_tok, 2 * out_row, 2 * (out_row - new_tok) + 1)
    order = jnp.where(in_row == wanted, 1.0, 0.0).astype(jnp.bfloat16)
    load_new.wait()
    all_new[z, x, head] = jnp.dot(
        order, new_ref[...], preferred_element_type=jnp.float32
    ).astype(jnp.bfloat16)
    load_q.wait()
    qz_ref[0] = q_ref[...].T
    ones = jnp.ones((16, chunk // PIECES), jnp.bfloat16)
    for part in range(heads_axis):
        for piece in range(PIECES):
            near_v[part, piece, pl.ds(size, 16), :] = ones
            far_v[part, piece, pl.ds(size, 16), :] = ones
    for load in small:
        load.wait()
    for number in range(slots):
        live = jnp.int32(0)
        for place in range(slots):
            hit = (table_ref[0, place] == number) & (place < count_ref[0])
            live = jnp.where(hit, jnp.int32(1), live)
        gap = jnp.where(live == 1, jnp.float32(0.0), jnp.float32(FAR))
        near_dead[pl.ds(8 * number, 8), :] = jnp.full((8, rows), gap, jnp.float32)
    load_k.wait()

    pl.semaphore_wait(barrier, layers + heads_axis - 1)

    def remote(src, dst, send_sem, recv_sem, device):
        return pltpu.make_async_remote_copy(
            src_ref=src,
            dst_ref=dst,
            send_sem=send_sem,
            recv_sem=recv_sem,
            device_id=device,
            device_id_type=MESH,
        )

    def place_values(part):
        for piece in range(PIECES):
            rows_in = pl.ds(piece * (chunk // PIECES), chunk // PIECES)
            near_v[part, piece, pl.ds(0, size), :] = v_ref[part, rows_in, :].T

    def send_q(steps):
        slot = layers - steps
        return remote(
            qz_ref.at[0],
            qz_ref.at[slot],
            qz_send.at[steps],
            qz_recv.at[slot],
            {"ctx": along_z(steps)},
        )

    def take_q(slot):
        return remote(
            qz_ref.at[0], qz_ref.at[slot], qz_send.at[slot], qz_recv.at[slot], {"ctx": along_z(slot)}
        )

    dead_over = remote(near_dead, far_dead, xd_send, xd_recv, {"ctx": pair})

    def key_piece(buffer, part, piece):
        return buffer.at[part, pl.ds(piece * (chunk // PIECES), chunk // PIECES)]

    def value_piece(buffer, part, piece):
        return buffer.at[part, piece, pl.ds(0, size)]

    def chip_part(owner, steps):
        return lax.rem(owner + 2 * steps, heads_axis)

    class Travel:
        def __init__(self, near, far, piece_of, sems):
            self.near, self.far, self.piece_of = near, far, piece_of
            self.x_send, self.x_recv, self.y_send, self.y_recv, self.c_send, self.c_recv = sems

        def over(self, piece):
            return remote(
                self.piece_of(self.near, head, piece),
                self.piece_of(self.far, head, piece),
                self.x_send.at[piece],
                self.x_recv.at[piece],
                {"ctx": pair},
            )

        def to_chip(self, piece, steps):
            mine = self.piece_of(self.far, head, piece)
            return remote(
                mine,
                mine,
                self.y_send.at[piece, steps],
                self.y_recv.at[piece, chips - steps],
                {"head": along_head(2 * steps)},
            )

        def from_chip(self, piece, steps):
            theirs = self.piece_of(self.far, chip_part(head, steps), piece)
            return remote(
                theirs,
                theirs,
                self.y_send.at[piece, steps],
                self.y_recv.at[piece, steps],
                {"head": along_head(2 * steps)},
            )

        def core(self, owner, piece, steps):
            block = self.piece_of(self.far, chip_part(owner, steps), piece)
            return remote(
                block,
                block,
                self.c_send.at[piece, steps],
                self.c_recv.at[piece, steps],
                {"head": other_core},
            )

        def spread(self, piece):
            self.over(piece).wait_recv()
            for steps in range(1, chips):
                self.to_chip(piece, steps).start()
            self.core(head, piece, 0).start()

        def spread_on(self, piece):
            for steps in range(1, chips):
                self.from_chip(piece, steps).wait_recv()
                self.core(head, piece, steps).start()

        def arrived(self):
            for piece in range(PIECES):
                for steps in range(chips):
                    self.core(other_core, piece, steps).wait_recv()

        def sent(self):
            for piece in range(PIECES):
                self.over(piece).wait_send()
                for steps in range(chips):
                    if steps:
                        self.to_chip(piece, steps).wait_send()
                    self.core(head, piece, steps).wait_send()

    key_sems = (xk_send, xk_recv, yk_send, yk_recv, ck_send, ck_recv)
    value_sems = (xv_send, xv_recv, yv_send, yv_recv, cv_send, cv_recv)
    keys = Travel(near_k, far_k, key_piece, key_sems)
    values = Travel(near_v, far_v, value_piece, value_sems)

    def give_back(steps):
        slot = layers - steps
        device = {"ctx": along_z(steps)}
        return (
            remote(sz_o.at[steps], rz_o.at[slot], zo_send.at[steps], zo_recv.at[slot], device),
            remote(sz_l.at[steps], rz_l.at[slot], zl_send.at[steps], zl_recv.at[slot], device),
        )

    def get_back(slot):
        device = {"ctx": along_z(slot)}
        return (
            remote(sz_o.at[slot], rz_o.at[slot], zo_send.at[slot], zo_recv.at[slot], device),
            remote(sz_l.at[slot], rz_l.at[slot], zl_send.at[slot], zl_recv.at[slot], device),
        )

    def new_z(steps):
        mine = all_new.at[z, x, head]
        return remote(
            mine, mine, nz_send.at[steps], nz_recv.at[layers - steps], {"ctx": along_z(steps)}
        )

    def new_z_taken(slot):
        theirs = all_new.at[lax.rem(z + slot, layers), x, head]
        return remote(theirs, theirs, nz_send.at[slot], nz_recv.at[slot], {"ctx": along_z(slot)})

    def new_x(parity):
        block = all_new.at[:, parity, head]
        return remote(block, block, nx_send, nx_recv, {"ctx": pair})

    def new_h(steps):
        mine = all_new.at[:, :, head]
        return remote(
            mine,
            mine,
            nh_send.at[steps],
            nh_recv.at[heads_axis - steps],
            {"head": along_head(steps)},
        )

    def new_h_taken(slot):
        theirs = all_new.at[:, :, along_head(slot)]
        return remote(
            theirs, theirs, nh_send.at[slot], nh_recv.at[slot], {"head": along_head(slot)}
        )

    for piece in range(PIECES):
        keys.over(piece).start()
    for steps in range(1, layers):
        send_q(steps).start()
    load_v.wait()
    place_values(head)
    for piece in range(PIECES):
        values.over(piece).start()
    dead_over.start()
    for steps in range(1, layers):
        new_z(steps).start()

    def partial(query_columns, keys, values, gaps):
        scores, top, dead = [], None, []
        for number in range(heads_axis):
            found = jnp.dot(keys[number], query_columns, preferred_element_type=jnp.float32)
            scores.append(found)
            dead.append(gaps[pl.ds(8 * (number // chunks_page), 1), :])
            page_top = jnp.max(found, axis=0, keepdims=True) - dead[number]
            top = page_top if top is None else jnp.maximum(top, page_top)
        summed = None
        for number in range(heads_axis):
            weights = jnp.exp2((scores[number] - (top + dead[number])) * scale)
            product = jnp.dot(
                jnp.concatenate([values[number, piece] for piece in range(PIECES)], axis=1),
                weights.astype(jnp.bfloat16),
                preferred_element_type=jnp.float32,
            )
            summed = product if summed is None else summed + product
        totals = summed[size : size + 1, :]
        return summed[:size, :] / totals, top * scale + jnp.log2(totals)

    def write(mean, level, mean_ref, level_ref):
        largest = jnp.max(jnp.abs(mean), axis=0, keepdims=True)
        steps = jnp.round(mean * (STEPS / jnp.maximum(largest, TINY)))
        mean_ref[...] = steps.astype(jnp.int32).astype(jnp.int16)
        line = lax.broadcasted_iota(jnp.int32, (8, rows), 0)
        level_ref[...] = jnp.where(line == 0, level, largest * (1.0 / STEPS))

    def read(mean_ref, level_ref):
        step = level_ref[1:2, :]
        return mean_ref[...].astype(jnp.int32).astype(jnp.float32) * step, level_ref[0:1, :]

    def merged(parts):
        top = functools.reduce(jnp.maximum, [level for _, level in parts])
        share = [jnp.exp2(level - top) for _, level in parts]
        whole = functools.reduce(jnp.add, share)
        summed = functools.reduce(jnp.add, [one * mean for one, (mean, _) in zip(share, parts)])
        return summed / whole, top + jnp.log2(whole)

    def near_step(slot):
        mean, level = partial(qz_ref[slot], near_k, near_v, near_dead)
        own_o[slot] = mean
        own_l[slot, 0:1, :] = level

    def far_step(slot):
        found = partial(qz_ref[slot], far_k, far_v, far_dead)
        return merged([(own_o[slot], own_l[slot, 0:1, :]), found])

    for step in range(1, heads_axis):
        place_values(along_head(step))
    near_step(0)
    keys.spread(0)

    def near_layer(slot, carry):
        take_q(slot).wait_recv()
        near_step(slot)

        @pl.when(slot == 1)
        def _():
            for other in range(1, layers):
                new_z_taken(other).wait_recv()
            new_x(x).start()

        for piece in range(1, PIECES):

            @pl.when(slot == piece)
            def _():
                keys.spread(piece)

        return carry

    lax.fori_loop(1, layers, near_layer, 0)
    new_x(1 - x).wait_recv()
    for steps in range(1, heads_axis):
        new_h(steps).start()
    keys.spread_on(0)
    for piece in range(PIECES):
        values.spread(piece)
        if piece < PIECES - 1:
            keys.spread_on(piece + 1)
        else:
            for later in range(PIECES):
                values.spread_on(later)

    for slot in range(1, heads_axis):
        new_h_taken(slot).wait_recv()
    tokens = layers * 2 * heads_axis * new_tok
    gathered = all_new[...].astype(jnp.float32).reshape(tokens // new_tok, 2, new_tok, size)
    new_keys = gathered[:, 0].reshape(tokens, size).astype(jnp.bfloat16)
    new_values = gathered[:, 1].reshape(tokens, size).astype(jnp.bfloat16)

    mine = owner_ref[...] == store
    target = jnp.where(mine, 2 * offset_ref[...], -2)
    place = lax.broadcasted_iota(jnp.int32, (appended_ref.shape[0], tokens), 0)
    key_rows = jnp.where(place == target, 1.0, 0.0).astype(jnp.bfloat16)
    value_rows = jnp.where(place == target + 1, 1.0, 0.0).astype(jnp.bfloat16)
    appended_ref[...] = (
        jnp.dot(key_rows, new_keys, preferred_element_type=jnp.float32)
        + jnp.dot(value_rows, new_values, preferred_element_type=jnp.float32)
    ).astype(jnp.bfloat16)

    scores = jnp.dot(new_keys, qz_ref[0], preferred_element_type=jnp.float32)
    token = lax.broadcasted_iota(jnp.int32, (tokens, rows), 0)
    asker = lax.broadcasted_iota(jnp.int32, (tokens, rows), 1)
    scores = jnp.where(token * head_dev - store * rows <= asker, scores, -FAR)
    top = jnp.max(scores, axis=0, keepdims=True)
    weights = jnp.exp2((scores - top) * scale)
    totals = jnp.sum(weights, axis=0, keepdims=True)
    summed = jnp.dot(
        new_values.T, weights.astype(jnp.bfloat16), preferred_element_type=jnp.float32
    )
    parts = [(summed / totals, top * scale + jnp.log2(totals))]

    dead_over.wait_recv()
    keys.arrived()
    values.arrived()

    def far_layer(number, carry):
        slot = 1 + lax.rem(number + layers // 2 - 1, layers - 1)
        mean, level = far_step(slot)
        write(mean, level, sz_o.at[slot], sz_l.at[slot])
        for copy in give_back(slot):
            copy.start()
        return carry

    lax.fori_loop(0, layers - 1, far_layer, 0)
    parts.append(far_step(0))
    for slot in range(1, layers):
        for copy in get_back(slot):
            copy.wait_recv()
        parts.append(read(rz_o.at[slot], rz_l.at[slot]))
    attended_ref[...] = merged(parts)[0].T.astype(jnp.bfloat16)

    dead_over.wait_send()
    keys.sent()
    values.sent()
    for slot in range(1, layers):
        send_q(slot).wait_send()
        new_z(slot).wait_send()
        for copy in give_back(slot):
            copy.wait_send()
    new_x(x).wait_send()
    for steps in range(1, heads_axis):
        new_h(steps).wait_send()


def shards(
    queries, cache_keys, cache_values, page_table, page_count, new_kv, new_owner, new_offset
):
    tok_dev, head_dev, size = queries.shape
    new_tok = new_kv.shape[0]
    slots = page_table.shape[1]
    stores = lax.axis_size("ctx")
    heads_axis = lax.axis_size("head")
    layers = stores // 2
    chunk = cache_keys.shape[0] // heads_axis
    rows = tok_dev * head_dev
    append_rows = 2 * tok_dev
    tokens = new_owner.shape[0]
    bf16, f32 = jnp.bfloat16, jnp.float32
    vmem = pl.BlockSpec(memory_space=pltpu.VMEM)
    smem = pl.BlockSpec(memory_space=pltpu.SMEM)
    hbm = pl.BlockSpec(memory_space=pltpu.HBM)
    mean_block = pltpu.VMEM((layers, size, rows), bf16)
    part_block = pltpu.VMEM((layers, size, rows), jnp.int16)
    level_block = pltpu.VMEM((layers, 8, rows), f32)
    dma = pltpu.SemaphoreType.DMA((layers,))
    attended, appended = pl.pallas_call(
        functools.partial(attention_kernel, layers, heads_axis, head_dev, slots),
        out_shape=(
            jax.ShapeDtypeStruct((rows, size), bf16),
            jax.ShapeDtypeStruct((2 * append_rows, size), bf16),
        ),
        in_specs=[hbm, smem] + [hbm] * 6,
        out_specs=(vmem, vmem),
        scratch_shapes=[
            pltpu.SMEM((1, slots), jnp.int32),
            pltpu.VMEM((2 * new_tok, size), bf16),
            pltpu.VMEM((1, tokens), jnp.int32),
            pltpu.VMEM((1, tokens), jnp.int32),
            pltpu.VMEM((rows, size), bf16),
            pltpu.VMEM((heads_axis, chunk, size), bf16),
            pltpu.VMEM((heads_axis, chunk, size), bf16),
            pltpu.VMEM((heads_axis, PIECES, size + 16, chunk // PIECES), bf16),
            pltpu.VMEM((heads_axis, chunk, size), bf16),
            pltpu.VMEM((heads_axis, PIECES, size + 16, chunk // PIECES), bf16),
            pltpu.VMEM((8 * slots, rows), f32),
            pltpu.VMEM((8 * slots, rows), f32),
            mean_block,
            pltpu.VMEM((layers, size, rows), f32),
            level_block,
            part_block,
            level_block,
            part_block,
            level_block,
            pltpu.VMEM((layers, 2, heads_axis, 2 * new_tok, size), bf16),
            pltpu.SemaphoreType.DMA((7,)),
        ]
        + [dma] * 2
        + [pltpu.SemaphoreType.DMA((PIECES,))] * 4
        + [pltpu.SemaphoreType.DMA] * 2
        + [pltpu.SemaphoreType.DMA((PIECES, heads_axis // 2))] * 8
        + [dma] * 6
        + [
            pltpu.SemaphoreType.DMA,
            pltpu.SemaphoreType.DMA,
            pltpu.SemaphoreType.DMA((heads_axis,)),
            pltpu.SemaphoreType.DMA((heads_axis,)),
        ],
        compiler_params=pltpu.CompilerParams(
            collective_id=0, has_side_effects=True, vmem_limit_bytes=62 * 1024 * 1024
        ),
    )(
        page_table,
        page_count,
        queries.reshape(rows, size),
        cache_keys.reshape(heads_axis, chunk, size),
        cache_values.reshape(heads_axis, chunk, size),
        new_kv.reshape(2 * new_tok, size),
        new_owner.reshape(1, tokens),
        new_offset.reshape(1, tokens),
    )
    return (
        attended.reshape(tok_dev, head_dev, size),
        appended.reshape(append_rows, 2, size),
    )


def solution(mesh):
    in_specs = (
        P("ctx", "head", None),
        P("ctx", None),
        P("ctx", None),
        P("ctx", None),
        P("ctx"),
        P(("ctx", "head"), None, None),
        P(),
        P(),
    )
    out_specs = (P("ctx", "head", None), P("ctx", None, None))
    return jax.shard_map(shards, mesh=mesh, in_specs=in_specs, out_specs=out_specs, check_vma=False)
```

```python
import functools
import math

import jax
import jax.numpy as jnp
from jax import lax
from jax.experimental import pallas as pl
from jax.experimental.pallas import tpu as pltpu
from jax.sharding import PartitionSpec as P

MESH = pl.DeviceIdType.MESH
FAR = 1e30
STEPS = 32767.0
TINY = 1e-30


def attention_kernel(
    layers,
    heads_axis,
    head_dev,
    slots,
    table_hbm,
    count_ref,
    queries_ref,
    keys_ref,
    values_ref,
    new_hbm,
    owner_hbm,
    offset_hbm,
    attended_ref,
    appended_ref,
    table_ref,
    new_ref,
    owner_ref,
    offset_ref,
    q_ref,
    k_ref,
    v_ref,
    vt_ref,
    qz_ref,
    qx_ref,
    own_o,
    own_l,
    sx_o,
    sx_l,
    rx_o,
    rx_l,
    sz_o,
    sz_l,
    rz_o,
    rz_l,
    all_new,
    local_sem,
    qz_send,
    qz_recv,
    qx_send,
    qx_recv,
    xo_send,
    xo_recv,
    xl_send,
    xl_recv,
    zo_send,
    zo_recv,
    zl_send,
    zl_recv,
    nz_send,
    nz_recv,
    nx_send,
    nx_recv,
    nh_send,
    nh_recv,
):
    rows, size = queries_ref.shape
    store_rows = keys_ref.shape[0]
    page = store_rows // slots
    new_tok = new_hbm.shape[0] // 2
    scale = math.log2(math.e) / math.sqrt(size)
    store = lax.axis_index("ctx")
    head = lax.axis_index("head")
    z = lax.div(store, 2)
    x = lax.rem(store, 2)
    pair = store + 1 - 2 * x

    def along_z(steps):
        return 2 * lax.rem(z + steps, layers) + x

    def along_head(steps):
        return lax.rem(head + steps, heads_axis)

    load_new = pltpu.make_async_copy(new_hbm, new_ref, local_sem.at[3])
    small = [
        pltpu.make_async_copy(table_hbm, table_ref, local_sem.at[4]),
        pltpu.make_async_copy(owner_hbm, owner_ref, local_sem.at[5]),
        pltpu.make_async_copy(offset_hbm, offset_ref, local_sem.at[6]),
    ]
    load_q = pltpu.make_async_copy(queries_ref, q_ref, local_sem.at[0])
    load_k = pltpu.make_async_copy(keys_ref, k_ref, local_sem.at[1])
    load_v = pltpu.make_async_copy(values_ref, v_ref, local_sem.at[2])
    load_q.start()
    load_new.start()
    load_k.start()
    load_v.start()
    for load in small:
        load.start()

    barrier = pltpu.get_barrier_semaphore()
    for steps in range(1, layers):
        pl.semaphore_signal(barrier, inc=1, device_id={"ctx": along_z(steps)}, device_id_type=MESH)
    pl.semaphore_signal(barrier, inc=1, device_id={"ctx": pair}, device_id_type=MESH)
    for steps in range(1, heads_axis):
        pl.semaphore_signal(
            barrier, inc=1, device_id={"head": along_head(steps)}, device_id_type=MESH
        )

    out_row = lax.broadcasted_iota(jnp.int32, (2 * new_tok, 2 * new_tok), 0)
    in_row = lax.broadcasted_iota(jnp.int32, (2 * new_tok, 2 * new_tok), 1)
    wanted = jnp.where(out_row < new_tok, 2 * out_row, 2 * (out_row - new_tok) + 1)
    order = jnp.where(in_row == wanted, 1.0, 0.0).astype(jnp.bfloat16)
    load_new.wait()
    all_new[z, x, head] = jnp.dot(
        order, new_ref[...], preferred_element_type=jnp.float32
    ).astype(jnp.bfloat16)
    load_q.wait()
    qz_ref[0] = q_ref[...].T

    pl.semaphore_wait(barrier, layers + heads_axis - 1)

    def remote(src, dst, send_sem, recv_sem, device):
        return pltpu.make_async_remote_copy(
            src_ref=src,
            dst_ref=dst,
            send_sem=send_sem,
            recv_sem=recv_sem,
            device_id=device,
            device_id_type=MESH,
        )

    def send_q(steps):
        slot = layers - steps
        return remote(
            qz_ref.at[0],
            qz_ref.at[slot],
            qz_send.at[steps],
            qz_recv.at[slot],
            {"ctx": along_z(steps)},
        )

    def take_q(slot):
        return remote(
            qz_ref.at[0], qz_ref.at[slot], qz_send.at[slot], qz_recv.at[slot], {"ctx": along_z(slot)}
        )

    def pass_q(slot):
        return remote(
            qz_ref.at[slot], qx_ref.at[slot], qx_send.at[slot], qx_recv.at[slot], {"ctx": pair}
        )

    first_pass = remote(
        qz_ref.at[0], qx_ref.at[0], qx_send.at[0], qx_recv.at[0], {"ctx": pair}
    )

    def cross(slot):
        return (
            remote(sx_o.at[slot], rx_o.at[slot], xo_send.at[slot], xo_recv.at[slot], {"ctx": pair}),
            remote(sx_l.at[slot], rx_l.at[slot], xl_send.at[slot], xl_recv.at[slot], {"ctx": pair}),
        )

    def give_back(steps):
        slot = layers - steps
        device = {"ctx": along_z(steps)}
        return (
            remote(sz_o.at[steps], rz_o.at[slot], zo_send.at[steps], zo_recv.at[slot], device),
            remote(sz_l.at[steps], rz_l.at[slot], zl_send.at[steps], zl_recv.at[slot], device),
        )

    def get_back(slot):
        device = {"ctx": along_z(slot)}
        return (
            remote(sz_o.at[slot], rz_o.at[slot], zo_send.at[slot], zo_recv.at[slot], device),
            remote(sz_l.at[slot], rz_l.at[slot], zl_send.at[slot], zl_recv.at[slot], device),
        )

    def new_z(steps):
        mine = all_new.at[z, x, head]
        return remote(
            mine, mine, nz_send.at[steps], nz_recv.at[layers - steps], {"ctx": along_z(steps)}
        )

    def new_z_taken(slot):
        theirs = all_new.at[lax.rem(z + slot, layers), x, head]
        return remote(theirs, theirs, nz_send.at[slot], nz_recv.at[slot], {"ctx": along_z(slot)})

    def new_x(parity):
        block = all_new.at[:, parity, head]
        return remote(block, block, nx_send, nx_recv, {"ctx": pair})

    def new_h(steps):
        mine = all_new.at[:, :, head]
        return remote(
            mine,
            mine,
            nh_send.at[steps],
            nh_recv.at[heads_axis - steps],
            {"head": along_head(steps)},
        )

    def new_h_taken(slot):
        theirs = all_new.at[:, :, along_head(slot)]
        return remote(
            theirs, theirs, nh_send.at[slot], nh_recv.at[slot], {"head": along_head(slot)}
        )

    first_pass.start()
    for steps in range(1, layers):
        send_q(steps).start()
    for steps in range(1, layers):
        new_z(steps).start()

    for load in small:
        load.wait()
    dead = []
    for number in range(slots):
        live = jnp.int32(0)
        for place in range(slots):
            hit = (table_ref[0, place] == number) & (place < count_ref[0])
            live = jnp.where(hit, jnp.int32(1), live)
        dead.append(jnp.where(live == 1, jnp.float32(0.0), jnp.float32(FAR)))

    def partial(query_columns):
        scores, top = [], None
        for number in range(slots):
            found = jnp.dot(
                k_ref[pl.ds(number * page, page), :],
                query_columns,
                preferred_element_type=jnp.float32,
            )
            scores.append(found)
            page_top = jnp.max(found, axis=0, keepdims=True) - dead[number]
            top = page_top if top is None else jnp.maximum(top, page_top)
        summed = None
        for number in range(slots):
            weights = jnp.exp2((scores[number] - (top + dead[number])) * scale)
            product = jnp.dot(
                vt_ref[:, pl.ds(number * page, page)],
                weights.astype(jnp.bfloat16),
                preferred_element_type=jnp.float32,
            )
            summed = product if summed is None else summed + product
        totals = summed[size : size + 1, :]
        return summed[:size, :] / totals, top * scale + jnp.log2(totals)

    def write(mean, level, mean_ref, level_ref):
        largest = jnp.max(jnp.abs(mean), axis=0, keepdims=True)
        steps = jnp.round(mean * (STEPS / jnp.maximum(largest, TINY)))
        mean_ref[...] = steps.astype(jnp.int32).astype(jnp.int16)
        line = lax.broadcasted_iota(jnp.int32, (8, rows), 0)
        level_ref[...] = jnp.where(line == 0, level, largest * (1.0 / STEPS))

    def read(mean_ref, level_ref):
        step = level_ref[1:2, :]
        return mean_ref[...].astype(jnp.int32).astype(jnp.float32) * step, level_ref[0:1, :]

    def merged(parts):
        top = functools.reduce(jnp.maximum, [level for _, level in parts])
        share = [jnp.exp2(level - top) for _, level in parts]
        whole = functools.reduce(jnp.add, share)
        summed = functools.reduce(jnp.add, [one * mean for one, (mean, _) in zip(share, parts)])
        return summed / whole, top + jnp.log2(whole)

    def join_pair(slot):
        for copy in cross(slot):
            copy.wait_recv()
        return merged(
            [
                (own_o[slot], own_l[slot, 0:1, :]),
                read(rx_o.at[slot], rx_l.at[slot]),
            ]
        )

    def send_joined(slot):
        mean, level = join_pair(slot)
        write(mean, level, sz_o.at[slot], sz_l.at[slot])
        for copy in give_back(slot):
            copy.start()

    def serve_pair(slot):
        mean, level = partial(qx_ref[slot])
        write(mean, level, sx_o.at[slot], sx_l.at[slot])
        for copy in cross(slot):
            copy.start()

    load_k.wait()
    load_v.wait()
    vt_ref[pl.ds(0, size), :] = v_ref[...].T
    vt_ref[pl.ds(size, 16), :] = jnp.ones((16, store_rows), jnp.bfloat16)
    mean, level = partial(qz_ref[0])
    own_o[0] = mean
    own_l[0, 0:1, :] = level
    first_pass.wait_recv()
    serve_pair(0)
    take_q(1).wait_recv()
    pass_q(1).start()

    def serve_own(slot):
        mean, level = partial(qz_ref[slot])
        own_o[slot] = mean
        own_l[slot, 0:1, :] = level

    def layer_step(slot, carry):
        serve_own(slot)
        take_q(slot + 1).wait_recv()
        pass_q(slot + 1).start()

        @pl.when(slot == 1)
        def _():
            for other in range(1, layers):
                new_z_taken(other).wait_recv()
            new_x(x).start()

        @pl.when(slot >= 2)
        def _():
            send_joined(slot - 1)

        pass_q(slot).wait_recv()
        serve_pair(slot)
        return carry

    last = layers - 1
    lax.fori_loop(1, last, layer_step, 0)
    new_x(1 - x).wait_recv()
    for steps in range(1, heads_axis):
        new_h(steps).start()
    pass_q(last).wait_recv()
    serve_pair(last)
    send_joined(last - 1)
    serve_own(last)
    send_joined(last)

    for slot in range(1, heads_axis):
        new_h_taken(slot).wait_recv()
    tokens = layers * 2 * heads_axis * new_tok
    gathered = all_new[...].astype(jnp.float32).reshape(tokens // new_tok, 2, new_tok, size)
    new_keys = gathered[:, 0].reshape(tokens, size).astype(jnp.bfloat16)
    new_values = gathered[:, 1].reshape(tokens, size).astype(jnp.bfloat16)

    mine = owner_ref[...] == store
    target = jnp.where(mine, 2 * offset_ref[...], -2)
    place = lax.broadcasted_iota(jnp.int32, (appended_ref.shape[0], tokens), 0)
    key_rows = jnp.where(place == target, 1.0, 0.0).astype(jnp.bfloat16)
    value_rows = jnp.where(place == target + 1, 1.0, 0.0).astype(jnp.bfloat16)
    appended_ref[...] = (
        jnp.dot(key_rows, new_keys, preferred_element_type=jnp.float32)
        + jnp.dot(value_rows, new_values, preferred_element_type=jnp.float32)
    ).astype(jnp.bfloat16)

    scores = jnp.dot(new_keys, qz_ref[0], preferred_element_type=jnp.float32)
    token = lax.broadcasted_iota(jnp.int32, (tokens, rows), 0)
    asker = lax.broadcasted_iota(jnp.int32, (tokens, rows), 1)
    scores = jnp.where(token * head_dev - store * rows <= asker, scores, -FAR)
    top = jnp.max(scores, axis=0, keepdims=True)
    weights = jnp.exp2((scores - top) * scale)
    totals = jnp.sum(weights, axis=0, keepdims=True)
    summed = jnp.dot(
        new_values.T, weights.astype(jnp.bfloat16), preferred_element_type=jnp.float32
    )
    parts = [(summed / totals, top * scale + jnp.log2(totals)), join_pair(0)]
    for slot in range(1, layers):
        for copy in get_back(slot):
            copy.wait_recv()
        parts.append(read(rz_o.at[slot], rz_l.at[slot]))
    attended_ref[...] = merged(parts)[0].T.astype(jnp.bfloat16)

    first_pass.wait_send()
    for slot in range(layers):
        for copy in cross(slot):
            copy.wait_send()
        if slot:
            send_q(slot).wait_send()
            pass_q(slot).wait_send()
            new_z(slot).wait_send()
            for copy in give_back(slot):
                copy.wait_send()
    new_x(x).wait_send()
    for steps in range(1, heads_axis):
        new_h(steps).wait_send()


def shards(
    queries, cache_keys, cache_values, page_table, page_count, new_kv, new_owner, new_offset
):
    tok_dev, head_dev, size = queries.shape
    new_tok = new_kv.shape[0]
    slots = page_table.shape[1]
    store_rows = cache_keys.shape[0]
    stores = lax.axis_size("ctx")
    heads_axis = lax.axis_size("head")
    layers = stores // 2
    rows = tok_dev * head_dev
    append_rows = 2 * tok_dev
    tokens = new_owner.shape[0]
    bf16, f32 = jnp.bfloat16, jnp.float32
    vmem = pl.BlockSpec(memory_space=pltpu.VMEM)
    smem = pl.BlockSpec(memory_space=pltpu.SMEM)
    hbm = pl.BlockSpec(memory_space=pltpu.HBM)
    mean_block = pltpu.VMEM((layers, size, rows), bf16)
    part_block = pltpu.VMEM((layers, size, rows), jnp.int16)
    level_block = pltpu.VMEM((layers, 8, rows), f32)
    dma = pltpu.SemaphoreType.DMA((layers,))
    attended, appended = pl.pallas_call(
        functools.partial(attention_kernel, layers, heads_axis, head_dev, slots),
        out_shape=(
            jax.ShapeDtypeStruct((rows, size), bf16),
            jax.ShapeDtypeStruct((2 * append_rows, size), bf16),
        ),
        in_specs=[hbm, smem] + [hbm] * 6,
        out_specs=(vmem, vmem),
        scratch_shapes=[
            pltpu.SMEM((1, slots), jnp.int32),
            pltpu.VMEM((2 * new_tok, size), bf16),
            pltpu.VMEM((1, tokens), jnp.int32),
            pltpu.VMEM((1, tokens), jnp.int32),
            pltpu.VMEM((rows, size), bf16),
            pltpu.VMEM((store_rows, size), bf16),
            pltpu.VMEM((store_rows, size), bf16),
            pltpu.VMEM((size + 16, store_rows), bf16),
            mean_block,
            mean_block,
            pltpu.VMEM((layers, size, rows), f32),
            level_block,
            part_block,
            level_block,
            part_block,
            level_block,
            part_block,
            level_block,
            part_block,
            level_block,
            pltpu.VMEM((layers, 2, heads_axis, 2 * new_tok, size), bf16),
            pltpu.SemaphoreType.DMA((7,)),
        ]
        + [dma] * 14
        + [
            pltpu.SemaphoreType.DMA,
            pltpu.SemaphoreType.DMA,
            pltpu.SemaphoreType.DMA((heads_axis,)),
            pltpu.SemaphoreType.DMA((heads_axis,)),
        ],
        compiler_params=pltpu.CompilerParams(
            collective_id=0, has_side_effects=True, vmem_limit_bytes=62 * 1024 * 1024
        ),
    )(
        page_table,
        page_count,
        queries.reshape(rows, size),
        cache_keys,
        cache_values,
        new_kv.reshape(2 * new_tok, size),
        new_owner.reshape(1, tokens),
        new_offset.reshape(1, tokens),
    )
    return (
        attended.reshape(tok_dev, head_dev, size),
        appended.reshape(append_rows, 2, size),
    )


def solution(mesh):
    in_specs = (
        P("ctx", "head", None),
        P("ctx", None),
        P("ctx", None),
        P("ctx", None),
        P("ctx"),
        P(("ctx", "head"), None, None),
        P(),
        P(),
    )
    out_specs = (P("ctx", "head", None), P("ctx", None, None))
    return jax.shard_map(shards, mesh=mesh, in_specs=in_specs, out_specs=out_specs, check_vma=False)
```

```python
import functools
import math

import jax
import jax.numpy as jnp
from jax import lax
from jax.experimental import pallas as pl
from jax.experimental.pallas import tpu as pltpu
from jax.sharding import PartitionSpec as P

MESH = pl.DeviceIdType.MESH
FAR = 1e30
STEPS = 32767.0
TINY = 1e-30


def attention_kernel(
    layers,
    heads_axis,
    head_dev,
    slots,
    table_hbm,
    count_ref,
    queries_ref,
    keys_ref,
    values_ref,
    new_hbm,
    owner_hbm,
    offset_hbm,
    attended_ref,
    appended_ref,
    table_ref,
    new_ref,
    owner_ref,
    offset_ref,
    q_ref,
    v_ref,
    near_k,
    near_v,
    far_k,
    far_v,
    near_dead,
    far_dead,
    score_ref,
    sum_ref,
    qz_ref,
    own_o,
    own_l,
    sz_o,
    sz_l,
    rz_o,
    rz_l,
    all_new,
    local_sem,
    qz_send,
    qz_recv,
    xk_send,
    xk_recv,
    xv_send,
    xv_recv,
    xd_send,
    xd_recv,
    yk_send,
    yk_recv,
    yv_send,
    yv_recv,
    ck_send,
    ck_recv,
    cv_send,
    cv_recv,
    zo_send,
    zo_recv,
    zl_send,
    zl_recv,
    nz_send,
    nz_recv,
    nx_send,
    nx_recv,
    nh_send,
    nh_recv,
):
    rows, size = queries_ref.shape
    chunk = keys_ref.shape[1]
    chunks_page = heads_axis // slots
    chips = heads_axis // 2
    new_tok = new_hbm.shape[0] // 2
    scale = math.log2(math.e) / math.sqrt(size)
    store = lax.axis_index("ctx")
    head = lax.axis_index("head")
    z = lax.div(store, 2)
    x = lax.rem(store, 2)
    pair = store + 1 - 2 * x
    core = lax.rem(head, 2)
    other_core = head + 1 - 2 * core

    def along_z(steps):
        return 2 * lax.rem(z + steps, layers) + x

    def along_head(steps):
        return lax.rem(head + steps, heads_axis)

    load_new = pltpu.make_async_copy(new_hbm, new_ref, local_sem.at[3])
    small = [
        pltpu.make_async_copy(table_hbm, table_ref, local_sem.at[4]),
        pltpu.make_async_copy(owner_hbm, owner_ref, local_sem.at[5]),
        pltpu.make_async_copy(offset_hbm, offset_ref, local_sem.at[6]),
    ]
    load_q = pltpu.make_async_copy(queries_ref, q_ref, local_sem.at[0])
    load_k = pltpu.make_async_copy(keys_ref, near_k, local_sem.at[1])
    load_v = pltpu.make_async_copy(values_ref, v_ref, local_sem.at[2])
    load_q.start()
    load_new.start()
    load_k.start()
    load_v.start()
    for load in small:
        load.start()

    barrier = pltpu.get_barrier_semaphore()
    for steps in range(1, layers):
        pl.semaphore_signal(barrier, inc=1, device_id={"ctx": along_z(steps)}, device_id_type=MESH)
    pl.semaphore_signal(barrier, inc=1, device_id={"ctx": pair}, device_id_type=MESH)
    for steps in range(1, heads_axis):
        pl.semaphore_signal(
            barrier, inc=1, device_id={"head": along_head(steps)}, device_id_type=MESH
        )

    out_row = lax.broadcasted_iota(jnp.int32, (2 * new_tok, 2 * new_tok), 0)
    in_row = lax.broadcasted_iota(jnp.int32, (2 * new_tok, 2 * new_tok), 1)
    wanted = jnp.where(out_row < new_tok, 2 * out_row, 2 * (out_row - new_tok) + 1)
    order = jnp.where(in_row == wanted, 1.0, 0.0).astype(jnp.bfloat16)
    load_new.wait()
    all_new[z, x, head] = jnp.dot(
        order, new_ref[...], preferred_element_type=jnp.float32
    ).astype(jnp.bfloat16)
    load_q.wait()
    qz_ref[0] = q_ref[...].T
    for part in range(heads_axis):
        near_v[part, pl.ds(size, 16), :] = jnp.ones((16, chunk), jnp.bfloat16)
        far_v[part, pl.ds(size, 16), :] = jnp.ones((16, chunk), jnp.bfloat16)
    for load in small:
        load.wait()
    for number in range(slots):
        live = jnp.int32(0)
        for place in range(slots):
            hit = (table_ref[0, place] == number) & (place < count_ref[0])
            live = jnp.where(hit, jnp.int32(1), live)
        gap = jnp.where(live == 1, jnp.float32(0.0), jnp.float32(FAR))
        near_dead[pl.ds(8 * number, 8), :] = jnp.full((8, rows), gap, jnp.float32)
    load_k.wait()

    pl.semaphore_wait(barrier, layers + heads_axis - 1)

    def remote(src, dst, send_sem, recv_sem, device):
        return pltpu.make_async_remote_copy(
            src_ref=src,
            dst_ref=dst,
            send_sem=send_sem,
            recv_sem=recv_sem,
            device_id=device,
            device_id_type=MESH,
        )

    def send_q(steps):
        slot = layers - steps
        return remote(
            qz_ref.at[0],
            qz_ref.at[slot],
            qz_send.at[steps],
            qz_recv.at[slot],
            {"ctx": along_z(steps)},
        )

    def take_q(slot):
        return remote(
            qz_ref.at[0], qz_ref.at[slot], qz_send.at[slot], qz_recv.at[slot], {"ctx": along_z(slot)}
        )

    keys_over = remote(near_k.at[head], far_k.at[head], xk_send, xk_recv, {"ctx": pair})
    values_over = remote(
        near_v.at[head, pl.ds(0, size)],
        far_v.at[head, pl.ds(0, size)],
        xv_send,
        xv_recv,
        {"ctx": pair},
    )
    dead_over = remote(near_dead, far_dead, xd_send, xd_recv, {"ctx": pair})

    def far_part(buffer, owner, steps):
        part = lax.rem(owner + 2 * steps, heads_axis)
        return buffer.at[part, pl.ds(0, buffer.shape[1] - (16 if buffer is far_v else 0))]

    def to_chip(buffer, send_sem, recv_sem, steps):
        mine = far_part(buffer, head, 0)
        device = {"head": along_head(2 * steps)}
        return remote(mine, mine, send_sem.at[steps], recv_sem.at[chips - steps], device)

    def from_chip(buffer, send_sem, recv_sem, steps):
        theirs = far_part(buffer, head, steps)
        device = {"head": along_head(2 * steps)}
        return remote(theirs, theirs, send_sem.at[steps], recv_sem.at[steps], device)

    def to_core(buffer, send_sem, recv_sem, steps):
        mine = far_part(buffer, head, steps)
        device = {"head": other_core}
        return remote(mine, mine, send_sem.at[steps], recv_sem.at[steps], device)

    def from_core(buffer, send_sem, recv_sem, steps):
        theirs = far_part(buffer, other_core, steps)
        device = {"head": other_core}
        return remote(theirs, theirs, send_sem.at[steps], recv_sem.at[steps], device)

    def spread(over, buffer, chip_sems, core_sems):
        over.wait_recv()
        for steps in range(1, chips):
            to_chip(buffer, *chip_sems, steps).start()
        to_core(buffer, *core_sems, 0).start()

    def spread_on(buffer, chip_sems, core_sems):
        for steps in range(1, chips):
            from_chip(buffer, *chip_sems, steps).wait_recv()
            to_core(buffer, *core_sems, steps).start()

    key_sems = ((yk_send, yk_recv), (ck_send, ck_recv))
    value_sems = ((yv_send, yv_recv), (cv_send, cv_recv))

    def give_back(steps):
        slot = layers - steps
        device = {"ctx": along_z(steps)}
        return (
            remote(sz_o.at[steps], rz_o.at[slot], zo_send.at[steps], zo_recv.at[slot], device),
            remote(sz_l.at[steps], rz_l.at[slot], zl_send.at[steps], zl_recv.at[slot], device),
        )

    def get_back(slot):
        device = {"ctx": along_z(slot)}
        return (
            remote(sz_o.at[slot], rz_o.at[slot], zo_send.at[slot], zo_recv.at[slot], device),
            remote(sz_l.at[slot], rz_l.at[slot], zl_send.at[slot], zl_recv.at[slot], device),
        )

    def new_z(steps):
        mine = all_new.at[z, x, head]
        return remote(
            mine, mine, nz_send.at[steps], nz_recv.at[layers - steps], {"ctx": along_z(steps)}
        )

    def new_z_taken(slot):
        theirs = all_new.at[lax.rem(z + slot, layers), x, head]
        return remote(theirs, theirs, nz_send.at[slot], nz_recv.at[slot], {"ctx": along_z(slot)})

    def new_x(parity):
        block = all_new.at[:, parity, head]
        return remote(block, block, nx_send, nx_recv, {"ctx": pair})

    def new_h(steps):
        mine = all_new.at[:, :, head]
        return remote(
            mine,
            mine,
            nh_send.at[steps],
            nh_recv.at[heads_axis - steps],
            {"head": along_head(steps)},
        )

    def new_h_taken(slot):
        theirs = all_new.at[:, :, along_head(slot)]
        return remote(
            theirs, theirs, nh_send.at[slot], nh_recv.at[slot], {"head": along_head(slot)}
        )

    keys_over.start()
    for steps in range(1, layers):
        send_q(steps).start()
    load_v.wait()
    near_v[head, pl.ds(0, size), :] = v_ref[head].T
    values_over.start()
    dead_over.start()
    for steps in range(1, layers):
        new_z(steps).start()

    def partial(query_columns, keys, values, gaps):
        def gap(number):
            first = pl.multiple_of(8 * lax.div(number, chunks_page), 8)
            return gaps[pl.ds(first, 8), :][0:1, :]

        def score(number, top):
            found = jnp.dot(keys[number], query_columns, preferred_element_type=jnp.float32)
            score_ref[number] = found
            return jnp.maximum(top, jnp.max(found, axis=0, keepdims=True) - gap(number))

        def weigh(number, carry):
            weights = jnp.exp2((score_ref[number] - (top + gap(number))) * scale)
            sum_ref[...] += jnp.dot(
                values[number], weights.astype(jnp.bfloat16), preferred_element_type=jnp.float32
            )
            return carry

        lowest = jnp.full((1, rows), -3.0 * FAR, jnp.float32)
        top = lax.fori_loop(0, heads_axis, score, lowest)
        sum_ref[...] = jnp.zeros_like(sum_ref)
        lax.fori_loop(0, heads_axis, weigh, 0)
        summed = sum_ref[...]
        totals = summed[size : size + 1, :]
        return summed[:size, :] / totals, top * scale + jnp.log2(totals)

    def write(mean, level, mean_ref, level_ref):
        largest = jnp.max(jnp.abs(mean), axis=0, keepdims=True)
        steps = jnp.round(mean * (STEPS / jnp.maximum(largest, TINY)))
        mean_ref[...] = steps.astype(jnp.int32).astype(jnp.int16)
        line = lax.broadcasted_iota(jnp.int32, (8, rows), 0)
        level_ref[...] = jnp.where(line == 0, level, largest * (1.0 / STEPS))

    def read(mean_ref, level_ref):
        step = level_ref[1:2, :]
        return mean_ref[...].astype(jnp.int32).astype(jnp.float32) * step, level_ref[0:1, :]

    def merged(parts):
        top = functools.reduce(jnp.maximum, [level for _, level in parts])
        share = [jnp.exp2(level - top) for _, level in parts]
        whole = functools.reduce(jnp.add, share)
        summed = functools.reduce(jnp.add, [one * mean for one, (mean, _) in zip(share, parts)])
        return summed / whole, top + jnp.log2(whole)

    def near_step(slot):
        mean, level = partial(qz_ref[slot], near_k, near_v, near_dead)
        own_o[slot] = mean
        own_l[slot, 0:1, :] = level

    def far_step(slot):
        found = partial(qz_ref[slot], far_k, far_v, far_dead)
        return merged([(own_o[slot], own_l[slot, 0:1, :]), found])

    for step in range(1, heads_axis):
        part = along_head(step)
        near_v[part, pl.ds(0, size), :] = v_ref[part].T
    def near_layer(slot, carry):
        @pl.when(slot >= 1)
        def _():
            take_q(slot).wait_recv()

        near_step(slot)

        @pl.when(slot == 0)
        def _():
            spread(keys_over, far_k, *key_sems)

        @pl.when(slot == 1)
        def _():
            for other in range(1, layers):
                new_z_taken(other).wait_recv()
            new_x(x).start()

        @pl.when(slot == 2)
        def _():
            spread(values_over, far_v, *value_sems)

        return carry

    lax.fori_loop(0, layers, near_layer, 0)
    new_x(1 - x).wait_recv()
    for steps in range(1, heads_axis):
        new_h(steps).start()
    spread_on(far_k, *key_sems)
    spread_on(far_v, *value_sems)

    for slot in range(1, heads_axis):
        new_h_taken(slot).wait_recv()
    tokens = layers * 2 * heads_axis * new_tok
    gathered = all_new[...].astype(jnp.float32).reshape(tokens // new_tok, 2, new_tok, size)
    new_keys = gathered[:, 0].reshape(tokens, size).astype(jnp.bfloat16)
    new_values = gathered[:, 1].reshape(tokens, size).astype(jnp.bfloat16)

    mine = owner_ref[...] == store
    target = jnp.where(mine, 2 * offset_ref[...], -2)
    place = lax.broadcasted_iota(jnp.int32, (appended_ref.shape[0], tokens), 0)
    key_rows = jnp.where(place == target, 1.0, 0.0).astype(jnp.bfloat16)
    value_rows = jnp.where(place == target + 1, 1.0, 0.0).astype(jnp.bfloat16)
    appended_ref[...] = (
        jnp.dot(key_rows, new_keys, preferred_element_type=jnp.float32)
        + jnp.dot(value_rows, new_values, preferred_element_type=jnp.float32)
    ).astype(jnp.bfloat16)

    scores = jnp.dot(new_keys, qz_ref[0], preferred_element_type=jnp.float32)
    token = lax.broadcasted_iota(jnp.int32, (tokens, rows), 0)
    asker = lax.broadcasted_iota(jnp.int32, (tokens, rows), 1)
    scores = jnp.where(token * head_dev - store * rows <= asker, scores, -FAR)
    top = jnp.max(scores, axis=0, keepdims=True)
    weights = jnp.exp2((scores - top) * scale)
    totals = jnp.sum(weights, axis=0, keepdims=True)
    summed = jnp.dot(
        new_values.T, weights.astype(jnp.bfloat16), preferred_element_type=jnp.float32
    )
    parts = [(summed / totals, top * scale + jnp.log2(totals))]

    dead_over.wait_recv()
    for steps in range(chips):
        from_core(far_k, ck_send, ck_recv, steps).wait_recv()
        from_core(far_v, cv_send, cv_recv, steps).wait_recv()

    def far_layer(number, carry):
        slot = lax.rem(number + 1, layers)
        mean, level = far_step(slot)

        @pl.when(slot >= 1)
        def _():
            write(mean, level, sz_o.at[slot], sz_l.at[slot])
            for copy in give_back(slot):
                copy.start()

        @pl.when(slot == 0)
        def _():
            own_o[0] = mean
            own_l[0, 0:1, :] = level

        return carry

    lax.fori_loop(0, layers, far_layer, 0)
    parts.append((own_o[0], own_l[0, 0:1, :]))
    for slot in range(1, layers):
        for copy in get_back(slot):
            copy.wait_recv()
        parts.append(read(rz_o.at[slot], rz_l.at[slot]))
    attended_ref[...] = merged(parts)[0].T.astype(jnp.bfloat16)

    for copy in (keys_over, values_over, dead_over):
        copy.wait_send()
    for steps in range(chips):
        if steps:
            to_chip(far_k, yk_send, yk_recv, steps).wait_send()
            to_chip(far_v, yv_send, yv_recv, steps).wait_send()
        to_core(far_k, ck_send, ck_recv, steps).wait_send()
        to_core(far_v, cv_send, cv_recv, steps).wait_send()
    for slot in range(1, layers):
        send_q(slot).wait_send()
        new_z(slot).wait_send()
        for copy in give_back(slot):
            copy.wait_send()
    new_x(x).wait_send()
    for steps in range(1, heads_axis):
        new_h(steps).wait_send()


def shards(
    queries, cache_keys, cache_values, page_table, page_count, new_kv, new_owner, new_offset
):
    tok_dev, head_dev, size = queries.shape
    new_tok = new_kv.shape[0]
    slots = page_table.shape[1]
    stores = lax.axis_size("ctx")
    heads_axis = lax.axis_size("head")
    layers = stores // 2
    chunk = cache_keys.shape[0] // heads_axis
    rows = tok_dev * head_dev
    append_rows = 2 * tok_dev
    tokens = new_owner.shape[0]
    bf16, f32 = jnp.bfloat16, jnp.float32
    vmem = pl.BlockSpec(memory_space=pltpu.VMEM)
    smem = pl.BlockSpec(memory_space=pltpu.SMEM)
    hbm = pl.BlockSpec(memory_space=pltpu.HBM)
    mean_block = pltpu.VMEM((layers, size, rows), bf16)
    part_block = pltpu.VMEM((layers, size, rows), jnp.int16)
    level_block = pltpu.VMEM((layers, 8, rows), f32)
    dma = pltpu.SemaphoreType.DMA((layers,))
    attended, appended = pl.pallas_call(
        functools.partial(attention_kernel, layers, heads_axis, head_dev, slots),
        out_shape=(
            jax.ShapeDtypeStruct((rows, size), bf16),
            jax.ShapeDtypeStruct((2 * append_rows, size), bf16),
        ),
        in_specs=[hbm, smem] + [hbm] * 6,
        out_specs=(vmem, vmem),
        scratch_shapes=[
            pltpu.SMEM((1, slots), jnp.int32),
            pltpu.VMEM((2 * new_tok, size), bf16),
            pltpu.VMEM((1, tokens), jnp.int32),
            pltpu.VMEM((1, tokens), jnp.int32),
            pltpu.VMEM((rows, size), bf16),
            pltpu.VMEM((heads_axis, chunk, size), bf16),
            pltpu.VMEM((heads_axis, chunk, size), bf16),
            pltpu.VMEM((heads_axis, size + 16, chunk), bf16),
            pltpu.VMEM((heads_axis, chunk, size), bf16),
            pltpu.VMEM((heads_axis, size + 16, chunk), bf16),
            pltpu.VMEM((8 * slots, rows), f32),
            pltpu.VMEM((8 * slots, rows), f32),
            pltpu.VMEM((heads_axis, chunk, rows), f32),
            pltpu.VMEM((size + 16, rows), f32),
            mean_block,
            pltpu.VMEM((layers, size, rows), f32),
            level_block,
            part_block,
            level_block,
            part_block,
            level_block,
            pltpu.VMEM((layers, 2, heads_axis, 2 * new_tok, size), bf16),
            pltpu.SemaphoreType.DMA((7,)),
        ]
        + [dma] * 2
        + [pltpu.SemaphoreType.DMA] * 6
        + [pltpu.SemaphoreType.DMA((heads_axis // 2,))] * 8
        + [dma] * 6
        + [
            pltpu.SemaphoreType.DMA,
            pltpu.SemaphoreType.DMA,
            pltpu.SemaphoreType.DMA((heads_axis,)),
            pltpu.SemaphoreType.DMA((heads_axis,)),
        ],
        compiler_params=pltpu.CompilerParams(
            collective_id=0, has_side_effects=True, vmem_limit_bytes=62 * 1024 * 1024
        ),
    )(
        page_table,
        page_count,
        queries.reshape(rows, size),
        cache_keys.reshape(heads_axis, chunk, size),
        cache_values.reshape(heads_axis, chunk, size),
        new_kv.reshape(2 * new_tok, size),
        new_owner.reshape(1, tokens),
        new_offset.reshape(1, tokens),
    )
    return (
        attended.reshape(tok_dev, head_dev, size),
        appended.reshape(append_rows, 2, size),
    )


def solution(mesh):
    in_specs = (
        P("ctx", "head", None),
        P("ctx", None),
        P("ctx", None),
        P("ctx", None),
        P("ctx"),
        P(("ctx", "head"), None, None),
        P(),
        P(),
    )
    out_specs = (P("ctx", "head", None), P("ctx", None, None))
    return jax.shard_map(shards, mesh=mesh, in_specs=in_specs, out_specs=out_specs, check_vma=False)
```

```python
import functools
import math

import jax
import jax.numpy as jnp
from jax import lax
from jax.experimental import pallas as pl
from jax.experimental.pallas import tpu as pltpu
from jax.sharding import PartitionSpec as P

MESH = pl.DeviceIdType.MESH
FAR = 1e30
STEPS = 32767.0
TINY = 1e-30


def attention_kernel(
    layers,
    heads_axis,
    head_dev,
    slots,
    table_hbm,
    count_ref,
    queries_ref,
    keys_ref,
    values_ref,
    new_hbm,
    owner_hbm,
    offset_hbm,
    attended_ref,
    appended_ref,
    table_ref,
    new_ref,
    owner_ref,
    offset_ref,
    q_ref,
    v_ref,
    near_k,
    near_v,
    far_k,
    far_v,
    near_dead,
    far_dead,
    qz_ref,
    own_o,
    own_l,
    sz_o,
    sz_l,
    rz_o,
    rz_l,
    all_new,
    local_sem,
    qz_send,
    qz_recv,
    xk_send,
    xk_recv,
    xv_send,
    xv_recv,
    xd_send,
    xd_recv,
    yk_send,
    yk_recv,
    yv_send,
    yv_recv,
    ck_send,
    ck_recv,
    cv_send,
    cv_recv,
    zo_send,
    zo_recv,
    zl_send,
    zl_recv,
    nz_send,
    nz_recv,
    nx_send,
    nx_recv,
    nh_send,
    nh_recv,
):
    rows, size = queries_ref.shape
    chunk = keys_ref.shape[1]
    chunks_page = heads_axis // slots
    chips = heads_axis // 2
    new_tok = new_hbm.shape[0] // 2
    scale = math.log2(math.e) / math.sqrt(size)
    store = lax.axis_index("ctx")
    head = lax.axis_index("head")
    z = lax.div(store, 2)
    x = lax.rem(store, 2)
    pair = store + 1 - 2 * x
    core = lax.rem(head, 2)
    other_core = head + 1 - 2 * core

    def along_z(steps):
        return 2 * lax.rem(z + steps, layers) + x

    def along_head(steps):
        return lax.rem(head + steps, heads_axis)

    load_new = pltpu.make_async_copy(new_hbm, new_ref, local_sem.at[3])
    small = [
        pltpu.make_async_copy(table_hbm, table_ref, local_sem.at[4]),
        pltpu.make_async_copy(owner_hbm, owner_ref, local_sem.at[5]),
        pltpu.make_async_copy(offset_hbm, offset_ref, local_sem.at[6]),
    ]
    load_q = pltpu.make_async_copy(queries_ref, q_ref, local_sem.at[0])
    load_k = pltpu.make_async_copy(keys_ref, near_k, local_sem.at[1])
    load_v = pltpu.make_async_copy(values_ref, v_ref, local_sem.at[2])
    load_q.start()
    load_new.start()
    load_k.start()
    load_v.start()
    for load in small:
        load.start()

    barrier = pltpu.get_barrier_semaphore()
    for steps in range(1, layers):
        pl.semaphore_signal(barrier, inc=1, device_id={"ctx": along_z(steps)}, device_id_type=MESH)
    pl.semaphore_signal(barrier, inc=1, device_id={"ctx": pair}, device_id_type=MESH)
    for steps in range(1, heads_axis):
        pl.semaphore_signal(
            barrier, inc=1, device_id={"head": along_head(steps)}, device_id_type=MESH
        )

    out_row = lax.broadcasted_iota(jnp.int32, (2 * new_tok, 2 * new_tok), 0)
    in_row = lax.broadcasted_iota(jnp.int32, (2 * new_tok, 2 * new_tok), 1)
    wanted = jnp.where(out_row < new_tok, 2 * out_row, 2 * (out_row - new_tok) + 1)
    order = jnp.where(in_row == wanted, 1.0, 0.0).astype(jnp.bfloat16)
    load_new.wait()
    all_new[z, x, head] = jnp.dot(
        order, new_ref[...], preferred_element_type=jnp.float32
    ).astype(jnp.bfloat16)
    load_q.wait()
    qz_ref[0] = q_ref[...].T
    for part in range(heads_axis):
        near_v[part, pl.ds(size, 16), :] = jnp.ones((16, chunk), jnp.bfloat16)
        far_v[part, pl.ds(size, 16), :] = jnp.ones((16, chunk), jnp.bfloat16)
    for load in small:
        load.wait()
    for number in range(slots):
        live = jnp.int32(0)
        for place in range(slots):
            hit = (table_ref[0, place] == number) & (place < count_ref[0])
            live = jnp.where(hit, jnp.int32(1), live)
        gap = jnp.where(live == 1, jnp.float32(0.0), jnp.float32(FAR))
        near_dead[pl.ds(8 * number, 8), :] = jnp.full((8, rows), gap, jnp.float32)
    load_k.wait()

    pl.semaphore_wait(barrier, layers + heads_axis - 1)

    def remote(src, dst, send_sem, recv_sem, device):
        return pltpu.make_async_remote_copy(
            src_ref=src,
            dst_ref=dst,
            send_sem=send_sem,
            recv_sem=recv_sem,
            device_id=device,
            device_id_type=MESH,
        )

    def send_q(steps):
        slot = layers - steps
        return remote(
            qz_ref.at[0],
            qz_ref.at[slot],
            qz_send.at[steps],
            qz_recv.at[slot],
            {"ctx": along_z(steps)},
        )

    def take_q(slot):
        return remote(
            qz_ref.at[0], qz_ref.at[slot], qz_send.at[slot], qz_recv.at[slot], {"ctx": along_z(slot)}
        )

    keys_over = remote(near_k.at[head], far_k.at[head], xk_send, xk_recv, {"ctx": pair})
    values_over = remote(
        near_v.at[head, pl.ds(0, size)],
        far_v.at[head, pl.ds(0, size)],
        xv_send,
        xv_recv,
        {"ctx": pair},
    )
    dead_over = remote(near_dead, far_dead, xd_send, xd_recv, {"ctx": pair})

    def far_part(buffer, owner, steps):
        part = lax.rem(owner + 2 * steps, heads_axis)
        return buffer.at[part, pl.ds(0, buffer.shape[1] - (16 if buffer is far_v else 0))]

    def to_chip(buffer, send_sem, recv_sem, steps):
        mine = far_part(buffer, head, 0)
        device = {"head": along_head(2 * steps)}
        return remote(mine, mine, send_sem.at[steps], recv_sem.at[chips - steps], device)

    def from_chip(buffer, send_sem, recv_sem, steps):
        theirs = far_part(buffer, head, steps)
        device = {"head": along_head(2 * steps)}
        return remote(theirs, theirs, send_sem.at[steps], recv_sem.at[steps], device)

    def to_core(buffer, send_sem, recv_sem, steps):
        mine = far_part(buffer, head, steps)
        device = {"head": other_core}
        return remote(mine, mine, send_sem.at[steps], recv_sem.at[steps], device)

    def from_core(buffer, send_sem, recv_sem, steps):
        theirs = far_part(buffer, other_core, steps)
        device = {"head": other_core}
        return remote(theirs, theirs, send_sem.at[steps], recv_sem.at[steps], device)

    def spread(over, buffer, chip_sems, core_sems):
        over.wait_recv()
        for steps in range(1, chips):
            to_chip(buffer, *chip_sems, steps).start()
        to_core(buffer, *core_sems, 0).start()

    def spread_on(buffer, chip_sems, core_sems):
        for steps in range(1, chips):
            from_chip(buffer, *chip_sems, steps).wait_recv()
            to_core(buffer, *core_sems, steps).start()

    key_sems = ((yk_send, yk_recv), (ck_send, ck_recv))
    value_sems = ((yv_send, yv_recv), (cv_send, cv_recv))

    def give_back(steps):
        slot = layers - steps
        device = {"ctx": along_z(steps)}
        return (
            remote(sz_o.at[steps], rz_o.at[slot], zo_send.at[steps], zo_recv.at[slot], device),
            remote(sz_l.at[steps], rz_l.at[slot], zl_send.at[steps], zl_recv.at[slot], device),
        )

    def get_back(slot):
        device = {"ctx": along_z(slot)}
        return (
            remote(sz_o.at[slot], rz_o.at[slot], zo_send.at[slot], zo_recv.at[slot], device),
            remote(sz_l.at[slot], rz_l.at[slot], zl_send.at[slot], zl_recv.at[slot], device),
        )

    def new_z(steps):
        mine = all_new.at[z, x, head]
        return remote(
            mine, mine, nz_send.at[steps], nz_recv.at[layers - steps], {"ctx": along_z(steps)}
        )

    def new_z_taken(slot):
        theirs = all_new.at[lax.rem(z + slot, layers), x, head]
        return remote(theirs, theirs, nz_send.at[slot], nz_recv.at[slot], {"ctx": along_z(slot)})

    def new_x(parity):
        block = all_new.at[:, parity, head]
        return remote(block, block, nx_send, nx_recv, {"ctx": pair})

    def new_h(steps):
        mine = all_new.at[:, :, head]
        return remote(
            mine,
            mine,
            nh_send.at[steps],
            nh_recv.at[heads_axis - steps],
            {"head": along_head(steps)},
        )

    def new_h_taken(slot):
        theirs = all_new.at[:, :, along_head(slot)]
        return remote(
            theirs, theirs, nh_send.at[slot], nh_recv.at[slot], {"head": along_head(slot)}
        )

    keys_over.start()
    for steps in range(1, layers):
        send_q(steps).start()
    load_v.wait()
    near_v[head, pl.ds(0, size), :] = v_ref[head].T
    values_over.start()
    dead_over.start()
    for steps in range(1, layers):
        new_z(steps).start()

    def partial(query_columns, keys, values, gaps):
        scores, top, dead = [], None, []
        for number in range(heads_axis):
            found = jnp.dot(keys[number], query_columns, preferred_element_type=jnp.float32)
            scores.append(found)
            dead.append(gaps[pl.ds(8 * (number // chunks_page), 1), :])
            page_top = jnp.max(found, axis=0, keepdims=True) - dead[number]
            top = page_top if top is None else jnp.maximum(top, page_top)
        summed = None
        for number in range(heads_axis):
            weights = jnp.exp2((scores[number] - (top + dead[number])) * scale)
            product = jnp.dot(
                values[number],
                weights.astype(jnp.bfloat16),
                preferred_element_type=jnp.float32,
            )
            summed = product if summed is None else summed + product
        totals = summed[size : size + 1, :]
        return summed[:size, :] / totals, top * scale + jnp.log2(totals)

    def write(mean, level, mean_ref, level_ref):
        largest = jnp.max(jnp.abs(mean), axis=0, keepdims=True)
        steps = jnp.round(mean * (STEPS / jnp.maximum(largest, TINY)))
        mean_ref[...] = steps.astype(jnp.int32).astype(jnp.int16)
        line = lax.broadcasted_iota(jnp.int32, (8, rows), 0)
        level_ref[...] = jnp.where(line == 0, level, largest * (1.0 / STEPS))

    def read(mean_ref, level_ref):
        step = level_ref[1:2, :]
        return mean_ref[...].astype(jnp.int32).astype(jnp.float32) * step, level_ref[0:1, :]

    def merged(parts):
        top = functools.reduce(jnp.maximum, [level for _, level in parts])
        share = [jnp.exp2(level - top) for _, level in parts]
        whole = functools.reduce(jnp.add, share)
        summed = functools.reduce(jnp.add, [one * mean for one, (mean, _) in zip(share, parts)])
        return summed / whole, top + jnp.log2(whole)

    def near_step(slot):
        mean, level = partial(qz_ref[slot], near_k, near_v, near_dead)
        own_o[slot] = mean
        own_l[slot, 0:1, :] = level

    def far_step(slot):
        found = partial(qz_ref[slot], far_k, far_v, far_dead)
        return merged([(own_o[slot], own_l[slot, 0:1, :]), found])

    for step in range(1, heads_axis):
        part = along_head(step)
        near_v[part, pl.ds(0, size), :] = v_ref[part].T
    near_step(0)
    spread(keys_over, far_k, *key_sems)

    def near_layer(slot, carry):
        take_q(slot).wait_recv()
        near_step(slot)

        @pl.when(slot == 1)
        def _():
            for other in range(1, layers):
                new_z_taken(other).wait_recv()
            new_x(x).start()

        @pl.when(slot == 2)
        def _():
            spread(values_over, far_v, *value_sems)

        return carry

    lax.fori_loop(1, layers, near_layer, 0)
    new_x(1 - x).wait_recv()
    for steps in range(1, heads_axis):
        new_h(steps).start()
    spread_on(far_k, *key_sems)
    spread_on(far_v, *value_sems)

    for slot in range(1, heads_axis):
        new_h_taken(slot).wait_recv()
    tokens = layers * 2 * heads_axis * new_tok
    gathered = all_new[...].astype(jnp.float32).reshape(tokens // new_tok, 2, new_tok, size)
    new_keys = gathered[:, 0].reshape(tokens, size).astype(jnp.bfloat16)
    new_values = gathered[:, 1].reshape(tokens, size).astype(jnp.bfloat16)

    mine = owner_ref[...] == store
    target = jnp.where(mine, 2 * offset_ref[...], -2)
    place = lax.broadcasted_iota(jnp.int32, (appended_ref.shape[0], tokens), 0)
    key_rows = jnp.where(place == target, 1.0, 0.0).astype(jnp.bfloat16)
    value_rows = jnp.where(place == target + 1, 1.0, 0.0).astype(jnp.bfloat16)
    appended_ref[...] = (
        jnp.dot(key_rows, new_keys, preferred_element_type=jnp.float32)
        + jnp.dot(value_rows, new_values, preferred_element_type=jnp.float32)
    ).astype(jnp.bfloat16)

    scores = jnp.dot(new_keys, qz_ref[0], preferred_element_type=jnp.float32)
    token = lax.broadcasted_iota(jnp.int32, (tokens, rows), 0)
    asker = lax.broadcasted_iota(jnp.int32, (tokens, rows), 1)
    scores = jnp.where(token * head_dev - store * rows <= asker, scores, -FAR)
    top = jnp.max(scores, axis=0, keepdims=True)
    weights = jnp.exp2((scores - top) * scale)
    totals = jnp.sum(weights, axis=0, keepdims=True)
    summed = jnp.dot(
        new_values.T, weights.astype(jnp.bfloat16), preferred_element_type=jnp.float32
    )
    parts = [(summed / totals, top * scale + jnp.log2(totals))]

    dead_over.wait_recv()
    for steps in range(chips):
        from_core(far_k, ck_send, ck_recv, steps).wait_recv()
        from_core(far_v, cv_send, cv_recv, steps).wait_recv()

    def far_layer(number, carry):
        slot = 1 + lax.rem(number + layers // 2 - 1, layers - 1)
        mean, level = far_step(slot)
        write(mean, level, sz_o.at[slot], sz_l.at[slot])
        for copy in give_back(slot):
            copy.start()
        return carry

    lax.fori_loop(0, layers - 1, far_layer, 0)
    parts.append(far_step(0))
    for slot in range(1, layers):
        for copy in get_back(slot):
            copy.wait_recv()
        parts.append(read(rz_o.at[slot], rz_l.at[slot]))
    attended_ref[...] = merged(parts)[0].T.astype(jnp.bfloat16)

    for copy in (keys_over, values_over, dead_over):
        copy.wait_send()
    for steps in range(chips):
        if steps:
            to_chip(far_k, yk_send, yk_recv, steps).wait_send()
            to_chip(far_v, yv_send, yv_recv, steps).wait_send()
        to_core(far_k, ck_send, ck_recv, steps).wait_send()
        to_core(far_v, cv_send, cv_recv, steps).wait_send()
    for slot in range(1, layers):
        send_q(slot).wait_send()
        new_z(slot).wait_send()
        for copy in give_back(slot):
            copy.wait_send()
    new_x(x).wait_send()
    for steps in range(1, heads_axis):
        new_h(steps).wait_send()


def shards(
    queries, cache_keys, cache_values, page_table, page_count, new_kv, new_owner, new_offset
):
    tok_dev, head_dev, size = queries.shape
    new_tok = new_kv.shape[0]
    slots = page_table.shape[1]
    stores = lax.axis_size("ctx")
    heads_axis = lax.axis_size("head")
    layers = stores // 2
    chunk = cache_keys.shape[0] // heads_axis
    rows = tok_dev * head_dev
    append_rows = 2 * tok_dev
    tokens = new_owner.shape[0]
    bf16, f32 = jnp.bfloat16, jnp.float32
    vmem = pl.BlockSpec(memory_space=pltpu.VMEM)
    smem = pl.BlockSpec(memory_space=pltpu.SMEM)
    hbm = pl.BlockSpec(memory_space=pltpu.HBM)
    mean_block = pltpu.VMEM((layers, size, rows), bf16)
    part_block = pltpu.VMEM((layers, size, rows), jnp.int16)
    level_block = pltpu.VMEM((layers, 8, rows), f32)
    dma = pltpu.SemaphoreType.DMA((layers,))
    attended, appended = pl.pallas_call(
        functools.partial(attention_kernel, layers, heads_axis, head_dev, slots),
        out_shape=(
            jax.ShapeDtypeStruct((rows, size), bf16),
            jax.ShapeDtypeStruct((2 * append_rows, size), bf16),
        ),
        in_specs=[hbm, smem] + [hbm] * 6,
        out_specs=(vmem, vmem),
        scratch_shapes=[
            pltpu.SMEM((1, slots), jnp.int32),
            pltpu.VMEM((2 * new_tok, size), bf16),
            pltpu.VMEM((1, tokens), jnp.int32),
            pltpu.VMEM((1, tokens), jnp.int32),
            pltpu.VMEM((rows, size), bf16),
            pltpu.VMEM((heads_axis, chunk, size), bf16),
            pltpu.VMEM((heads_axis, chunk, size), bf16),
            pltpu.VMEM((heads_axis, size + 16, chunk), bf16),
            pltpu.VMEM((heads_axis, chunk, size), bf16),
            pltpu.VMEM((heads_axis, size + 16, chunk), bf16),
            pltpu.VMEM((8 * slots, rows), f32),
            pltpu.VMEM((8 * slots, rows), f32),
            mean_block,
            pltpu.VMEM((layers, size, rows), f32),
            level_block,
            part_block,
            level_block,
            part_block,
            level_block,
            pltpu.VMEM((layers, 2, heads_axis, 2 * new_tok, size), bf16),
            pltpu.SemaphoreType.DMA((7,)),
        ]
        + [dma] * 2
        + [pltpu.SemaphoreType.DMA] * 6
        + [pltpu.SemaphoreType.DMA((heads_axis // 2,))] * 8
        + [dma] * 6
        + [
            pltpu.SemaphoreType.DMA,
            pltpu.SemaphoreType.DMA,
            pltpu.SemaphoreType.DMA((heads_axis,)),
            pltpu.SemaphoreType.DMA((heads_axis,)),
        ],
        compiler_params=pltpu.CompilerParams(
            collective_id=0, has_side_effects=True, vmem_limit_bytes=62 * 1024 * 1024
        ),
    )(
        page_table,
        page_count,
        queries.reshape(rows, size),
        cache_keys.reshape(heads_axis, chunk, size),
        cache_values.reshape(heads_axis, chunk, size),
        new_kv.reshape(2 * new_tok, size),
        new_owner.reshape(1, tokens),
        new_offset.reshape(1, tokens),
    )
    return (
        attended.reshape(tok_dev, head_dev, size),
        appended.reshape(append_rows, 2, size),
    )


def solution(mesh):
    in_specs = (
        P("ctx", "head", None),
        P("ctx", None),
        P("ctx", None),
        P("ctx", None),
        P("ctx"),
        P(("ctx", "head"), None, None),
        P(),
        P(),
    )
    out_specs = (P("ctx", "head", None), P("ctx", None, None))
    return jax.shard_map(shards, mesh=mesh, in_specs=in_specs, out_specs=out_specs, check_vma=False)
```
